768 devices in a mesh: blk: 96 (over x, z, core), rep: 8 (over y).
Axes of the slice: x: 4, y: 8, z: 12, core: 2. Of those that a mesh axis runs over, the one named last changes fastest.
Arguments:
- grad_out: bfloat16 [12288, 1024], P('blk'), may hold values from -6 to 6
- agg_hidden: bfloat16 [12288, 1024], P('blk', 'rep'), may hold values from -6 to 6
- pre_hidden: bfloat16 [12288, 1024], P('blk', 'rep'), may hold values from -6 to 6
- agg_input: bfloat16 [12288, 512], P('blk'), may hold values from -6 to 6
- weight_in: bfloat16 [512, 1024], P(None, 'rep'), may hold values from -0.25 to 0.25
- weight_out: bfloat16 [1024, 1024], P('rep'), may hold values from -0.1875 to 0.1875
- edge_tiles: bfloat16 [96, 64, 128, 128], P('blk'), may hold values from -0.5 to 0.5
- tile_source: int32 [96, 64], P('blk'), may hold values from 0 to 95, as said below
- tile_count: int32 [96], P('blk'), may hold values from 1 to 64, as said below
- degree: int32 [12288], P('blk'), may hold values from 1 to 16
Outputs:
- grad_w_out: float32 [1024, 1024], P('rep')
- grad_w_in: float32 [512, 1024], P(None, 'rep')
- grad_input: float32 [12288, 512], P('blk')
The draws below stay inside these ranges and needn't reach their ends.
Inputs may be any that keep to these rules, and one draw needn't show every extreme that they name: `tile_source`: within one row block's list the 64 entries are distinct; slots at or after tile_count are ignored. `tile_count`: some row block has all 64 slots live.
All inputs are finite; a program needn't handle non-finite values.
Results may differ from the reference program's by a relative error of at most 0.011.
Values may be sent and summed in bfloat16 or wider, within the bound.
No kernel may reach another device: no remote copies, remote signals or barrier semaphores. Data moves between devices by JAX's collectives and lax.ppermute only.
A program may use at most 32 MiB of HBM per device.

```python
import jax
import jax.numpy as jnp
from jax import lax

FIN = 512
HID = 1024
TILE = 128
NBLK = 96
NODES = 12288
MAXT = 64


def draw_tile_source(key, part):
    key = jax.random.fold_in(key, 11)
    row_keys = jax.random.split(key, NBLK)
    orders = jax.vmap(lambda one_key: jax.random.permutation(one_key, NBLK))(row_keys)
    return orders[:, :MAXT].astype(jnp.int32)


def draw_tile_count(key, part):
    key = jax.random.fold_in(key, 23)
    first_key, second_key, third_key = jax.random.split(key, 3)
    first = jax.random.randint(first_key, (NBLK,), 1, MAXT + 1)
    second = jax.random.randint(second_key, (NBLK,), 1, MAXT + 1)
    counts = jnp.maximum(1, first * second // MAXT)
    chosen = jax.random.randint(third_key, (), 0, NBLK)
    counts = jnp.where(jnp.arange(NBLK) == chosen, MAXT, counts)
    return counts.astype(jnp.int32)


def with_ends(array, rng, least, largest):
    extent = array.shape
    index_at = [jax.random.randint(jax.random.fold_in(rng, axis), (), 0, extent[axis]) for axis in range(len(extent))]
    array = array.at[tuple(index_at)].set(least)
    longest = extent.index(max(extent))
    index_at[longest] = (index_at[longest] + 1) % extent[longest]
    return array.at[tuple(index_at)].set(largest)


def levels(own_key, shape, cuts, low, largest):
    loudness = 1.0
    for axis_at, parts in cuts:
        heights = jax.random.uniform(jax.random.fold_in(jax.random.fold_in(own_key, 6), axis_at), (parts,), jnp.float32, low / len(cuts), largest / len(cuts))
        loudness = loudness * jnp.repeat(jnp.exp(heights), shape[axis_at] // parts).reshape((-1,) + (1,) * (len(shape) - 1 - axis_at))
    return loudness


def centred(stream_key, extent, scale, bound, cuts=(), kind=jnp.bfloat16):
    entries = jax.random.normal(stream_key, extent, jnp.float32) * scale
    if len(cuts) > 0:
        entries = levels(stream_key, extent, cuts, -0.22, 0.18) * entries
    return jnp.clip(entries, min=-bound, max=bound).astype(kind)


def setup_inputs(seed: int = 0) -> dict:
    streams_of = jax.random.split(jax.random.key(seed), 11)
    grad_out = centred(streams_of[0], (NODES, HID), 1.0, 6.0, ((0, 96),))
    agg_hidden = centred(streams_of[1], (NODES, HID), 1.0, 6.0, ((0, 96), (1, 8)))
    pre_hidden = centred(streams_of[2], (NODES, HID), 1.0, 6.0, ((0, 96), (1, 8)))
    agg_input = centred(streams_of[3], (NODES, FIN), 1.0, 6.0, ((0, 96),))
    weight_in = centred(streams_of[4], (FIN, HID), FIN ** -0.5, 0.25, ((1, 8),))
    weight_out = centred(streams_of[5], (HID, HID), HID ** -0.5, 0.1875, ((0, 8),))
    edge_tiles = centred(streams_of[6], (NBLK, MAXT, TILE, TILE), TILE ** -0.5, 0.5, ((0, 96),))
    tile_source = draw_tile_source(jax.random.fold_in(streams_of[10], 71), 0)
    tile_count = draw_tile_count(jax.random.fold_in(streams_of[10], 71), 0)
    degree = with_ends(jax.random.randint(streams_of[9], (NODES,), 1, 17), jax.random.fold_in(streams_of[9], 1), 1, 16).astype(jnp.int32)
    return dict(grad_out=grad_out, agg_hidden=agg_hidden, pre_hidden=pre_hidden, agg_input=agg_input, weight_in=weight_in, weight_out=weight_out, edge_tiles=edge_tiles, tile_source=tile_source, tile_count=tile_count, degree=degree)


def propagate(payload, inv_root, edge_tiles, tile_source, tile_count):
    blocks = payload.reshape(NBLK, TILE, payload.shape[1])

    def per_block(members):
        tile_row, source_row, live_count = members
        active = jnp.arange(MAXT, dtype=jnp.int32) < live_count
        picked = jnp.take(blocks, source_row, axis=0).astype(jnp.float32)
        masked = jnp.where(active[:, None, None], tile_row.astype(jnp.float32), jnp.zeros((), jnp.float32))
        return jnp.einsum('tij,tjk->ik', masked, picked)
    summed = lax.map(per_block, (edge_tiles, tile_source, tile_count))
    return summed.reshape(NODES, payload.shape[1]) * inv_root

def reference(grad_out, agg_hidden, pre_hidden, agg_input, weight_in, weight_out, edge_tiles, tile_source, tile_count, degree):
    inv_root = (1.0 / jnp.sqrt(degree.astype(jnp.float32)))[:, None]
    grad_w_out = jnp.dot(agg_hidden.T, grad_out, preferred_element_type=jnp.float32)
    delta_agg = jnp.dot(grad_out, weight_out.T, preferred_element_type=jnp.float32)
    scaled_out = (inv_root * delta_agg).astype(jnp.bfloat16)
    grad_hidden = propagate(scaled_out, inv_root, edge_tiles, tile_source, tile_count)
    grad_pre = jnp.where(pre_hidden > 0, grad_hidden, jnp.zeros((), jnp.float32)).astype(jnp.bfloat16)
    scaled_pre = (inv_root * grad_pre.astype(jnp.float32)).astype(jnp.bfloat16)
    grad_w_in = jnp.dot(agg_input.T, grad_pre, preferred_element_type=jnp.float32)
    spread = propagate(scaled_pre, inv_root, edge_tiles, tile_source, tile_count).astype(jnp.bfloat16)
    grad_input = jnp.dot(spread, weight_in.T, preferred_element_type=jnp.float32)
    return (grad_w_out, grad_w_in, grad_input)
```

```python
import jax
import jax.numpy as jnp
from jax import lax
from jax.experimental import pallas as pl
from jax.experimental.pallas import tpu as pltpu
from jax.sharding import PartitionSpec as P

TILE = 128
NX, NZ, NC = 4, 12, 2
NREP = 8
SLOTS = 64
STEP = 8
BF16 = jnp.bfloat16
F32 = jnp.float32
VMEM_LIMIT = 48 * 1024 * 1024


def blk_index(x, z, c):
    return (x * NZ + z) * NC + c


Z_GROUPS = [[blk_index(x, z, c) for z in range(NZ)] for x in range(NX) for c in range(NC)]
X_GROUPS = [[blk_index(x, z, c) for x in range(NX)] for z in range(NZ) for c in range(NC)]
CORE_SWAP = [(i, i ^ 1) for i in range(NX * NZ * NC)]


def vmem():
    return pl.BlockSpec(memory_space=pltpu.VMEM)


def smem():
    return pl.BlockSpec(memory_space=pltpu.SMEM)


def call(kernel, out_shape, in_specs, flops, moved):
    return pl.pallas_call(
        kernel,
        out_shape=out_shape,
        in_specs=in_specs,
        out_specs=jax.tree.map(lambda _: vmem(), out_shape),
        compiler_params=pltpu.CompilerParams(vmem_limit_bytes=VMEM_LIMIT),
        cost_estimate=pl.CostEstimate(flops=flops, bytes_accessed=moved, transcendentals=0),
    )


def column_scale(degree_ref):
    inv_root = 1.0 / jnp.sqrt(degree_ref[...].astype(F32))
    return jnp.broadcast_to(inv_root, (TILE, TILE)).T


def scale_out_kernel(degree_ref, grad_out_ref, weight_out_ref, out_ref):
    delta = lax.dot_general(
        grad_out_ref[...], weight_out_ref[...], (((1,), (1,)), ((), ())), preferred_element_type=F32
    )
    scaled = (column_scale(degree_ref) * delta).astype(BF16)
    for j in range(NZ):
        out_ref[j] = scaled


def sum_tiles(core_ref, source_ref, count_ref, mine_ref, theirs_ref, tiles_ref, extra):
    core, count = core_ref[0], count_ref[0]

    def step(s, total):
        left, right = [], []
        for k in range(STEP):
            slot = s * STEP + k
            source = source_ref[0, slot]
            chip = lax.shift_right_logical(source, 1)
            place = chip + extra * lax.div(chip, NZ)
            block = jnp.where((source & 1) == core, mine_ref[place], theirs_ref[place])
            right.append(jnp.where(slot < count, block, jnp.zeros_like(block)))
            left.append(tiles_ref[0, slot])
        return total + jnp.dot(
            jnp.concatenate(left, axis=1), jnp.concatenate(right, axis=0), preferred_element_type=F32
        )

    steps = lax.div(count + (STEP - 1), STEP)
    return lax.fori_loop(0, steps, step, jnp.zeros((TILE, TILE), F32))


def hidden_kernel(
    core_ref,
    source_ref,
    count_ref,
    degree_ref,
    mine_ref,
    theirs_ref,
    tiles_ref,
    pre_hidden_ref,
    agg_hidden_ref,
    grad_out_ref,
    agg_input_ref,
    out_ref,
):
    scale = column_scale(degree_ref)
    summed = sum_tiles(core_ref, source_ref, count_ref, mine_ref, theirs_ref, tiles_ref, 0)
    grad_pre = jnp.where(pre_hidden_ref[...].astype(F32) > 0, scale * summed, 0.0).astype(BF16)
    scaled_pre = (scale * grad_pre.astype(F32)).astype(BF16)
    for j in range(NZ):
        out_ref[j, :TILE] = scaled_pre
    across = (((0,), (0,)), ((), ()))
    w_out = lax.dot_general(agg_hidden_ref[...], grad_out_ref[...], across, preferred_element_type=F32)
    for j in range(8):
        out_ref[j, TILE:] = w_out[:, j * TILE : (j + 1) * TILE].astype(BF16)
    w_in = lax.dot_general(agg_input_ref[...], grad_pre, across, preferred_element_type=F32)
    for j in range(4):
        out_ref[8 + j, TILE:] = w_in[j * TILE : (j + 1) * TILE].astype(BF16)


def row_sum_kernel(got_ref, out_ref):
    total = got_ref[0, TILE:].astype(F32)
    for j in range(1, NZ):
        total = total + got_ref[j, TILE:].astype(F32)
    total = total.astype(BF16)
    for i in range(NX):
        for j in range(NZ):
            out_ref[i, j] = got_ref[j, :TILE]
        out_ref[i, NZ] = total


def spread_kernel(
    core_ref, source_ref, count_ref, degree_ref, mine_ref, theirs_ref, tiles_ref, spread_ref, weight_ref
):
    summed = sum_tiles(core_ref, source_ref, count_ref, mine_ref, theirs_ref, tiles_ref, 1)
    spread = (column_scale(degree_ref) * summed).astype(BF16)
    for j in range(NREP):
        spread_ref[j] = spread
    total = jnp.zeros((TILE, TILE), F32)
    for i in range(NX):
        at = i * (NZ + 1) + NZ
        total = total + (mine_ref[at].astype(F32) + theirs_ref[at].astype(F32))
    total = total.astype(BF16)
    for j in range(NZ):
        weight_ref[j] = total


def final_kernel(weights_ref, spread_ref, weight_in_ref, w_out_ref, w_in_ref, input_ref):
    for j in range(8):
        w_out_ref[:, j * TILE : (j + 1) * TILE] = weights_ref[j].astype(F32)
    for j in range(4):
        w_in_ref[j * TILE : (j + 1) * TILE] = weights_ref[8 + j].astype(F32)
    total = jnp.zeros((TILE, 512), F32)
    for k in range(NREP):
        total = total + lax.dot_general(
            spread_ref[k], weight_in_ref[k], (((1,), (1,)), ((), ())), preferred_element_type=F32
        )
    input_ref[...] = total


def local(
    grad_out,
    agg_hidden,
    pre_hidden,
    agg_input,
    weight_in,
    weight_out,
    edge_tiles,
    tile_source,
    tile_count,
    degree,
):
    shape = jax.ShapeDtypeStruct
    core = (lax.axis_index("blk") % 2).astype(jnp.int32).reshape(1)
    degree = degree.reshape(1, TILE)
    with jax.named_scope("weight_in_gather"):
        weights_in = lax.all_gather(weight_in, "rep", axis=0, tiled=False)

    with jax.named_scope("scale_out"):
        sent = call(
            scale_out_kernel, shape((NZ, TILE, TILE), BF16), [vmem()] * 3, 2 * 128 * 128 * 1024, 900000
        )(degree, grad_out, weight_out)
    with jax.named_scope("gather_out_z"):
        row = lax.all_to_all(sent, "blk", 0, 0, tiled=True, axis_index_groups=Z_GROUPS)
    with jax.named_scope("gather_out_x"):
        row = jnp.broadcast_to(row[None], (NX, NZ, TILE, TILE))
        mine = lax.all_to_all(row, "blk", 0, 0, tiled=True, axis_index_groups=X_GROUPS)
        mine = mine.reshape(NX * NZ, TILE, TILE)
    with jax.named_scope("gather_out_core"):
        theirs = lax.ppermute(mine, "blk", CORE_SWAP)
    theirs, weights_in = lax.optimization_barrier((theirs, weights_in))

    with jax.named_scope("hidden"):
        sent = call(
            hidden_kernel,
            shape((NZ, 2 * TILE, TILE), BF16),
            [smem()] * 3 + [vmem()] * 8,
            2 * 128 * 128 * 128 * 76,
            6000000,
        )(core, tile_source, tile_count, degree, mine, theirs, edge_tiles, pre_hidden, agg_hidden, grad_out, agg_input)
    with jax.named_scope("gather_pre_z"):
        row = lax.all_to_all(sent, "blk", 0, 0, tiled=True, axis_index_groups=Z_GROUPS)
    with jax.named_scope("row_sum"):
        row = call(row_sum_kernel, shape((NX, NZ + 1, TILE, TILE), BF16), [vmem()], 200000, 2500000)(row)
    with jax.named_scope("gather_pre_x"):
        mine = lax.all_to_all(row, "blk", 0, 0, tiled=True, axis_index_groups=X_GROUPS)
        mine = mine.reshape(NX * (NZ + 1), TILE, TILE)
    with jax.named_scope("gather_pre_core"):
        theirs = lax.ppermute(mine, "blk", CORE_SWAP)

    with jax.named_scope("spread"):
        spread, weights = call(
            spread_kernel,
            [shape((NREP, TILE, TILE), BF16), shape((NZ, TILE, TILE), BF16)],
            [smem()] * 3 + [vmem()] * 4,
            2 * 128 * 128 * 128 * 64,
            6000000,
        )(core, tile_source, tile_count, degree, mine, theirs, edge_tiles)
    with jax.named_scope("gather_spread"):
        spread = lax.all_to_all(spread, "rep", 0, 0, tiled=True)
    with jax.named_scope("gather_weights_z"):
        weights = lax.all_to_all(weights, "blk", 0, 0, tiled=True, axis_index_groups=Z_GROUPS)
    with jax.named_scope("final"):
        return tuple(
            call(
                final_kernel,
                [shape((128, 1024), F32), shape((512, 128), F32), shape((128, 512), F32)],
                [vmem()] * 3,
                2 * 128 * 1024 * 512,
                2500000,
            )(weights, spread, weights_in)
        )


def solution(mesh):
    return jax.shard_map(
        local,
        mesh=mesh,
        in_specs=(
            P("blk", None),
            P("blk", "rep"),
            P("blk", "rep"),
            P("blk", None),
            P(None, "rep"),
            P("rep", None),
            P("blk", None, None, None),
            P("blk", None),
            P("blk"),
            P("blk"),
        ),
        out_specs=(P("rep", None), P(None, "rep"), P("blk", None)),
        check_vma=False,
    )
```

```python
import jax
import jax.numpy as jnp
from jax import lax
from jax.experimental import pallas as pl
from jax.experimental.pallas import tpu as pltpu
from jax.sharding import PartitionSpec as P

TILE = 128
NX, NZ, NC = 4, 12, 2
NREP = 8
LINE = NZ * NC
WIDE = LINE * TILE
BF16 = jnp.bfloat16
F32 = jnp.float32
VMEM_LIMIT = 40 * 1024 * 1024
ACROSS = (((0,), (0,)), ((), ()))
BY_ROWS = (((1,), (1,)), ((), ()))


def blk_index(x, z, c):
    return (x * NZ + z) * NC + c


Z_GROUPS = [[blk_index(x, z, c) for z in range(NZ)] for x in range(NX) for c in range(NC)]
X_GROUPS = [[blk_index(x, z, c) for x in range(NX)] for z in range(NZ) for c in range(NC)]
LINE_GROUPS = [[x * LINE + p for p in range(LINE)] for x in range(NX)]


def along_x(k):
    return [(x * LINE + p, (x + k) % NX * LINE + p) for x in range(NX) for p in range(LINE)]


def vmem():
    return pl.BlockSpec(memory_space=pltpu.VMEM)


def smem():
    return pl.BlockSpec(memory_space=pltpu.SMEM)


def call(kernel, out_shape, in_specs, flops, moved):
    return pl.pallas_call(
        kernel,
        out_shape=out_shape,
        in_specs=in_specs,
        out_specs=jax.tree.map(lambda _: vmem(), out_shape),
        compiler_params=pltpu.CompilerParams(vmem_limit_bytes=VMEM_LIMIT),
        cost_estimate=pl.CostEstimate(flops=flops, bytes_accessed=moved, transcendentals=0),
    )


def column_scale(degree_ref):
    inv_root = 1.0 / jnp.sqrt(degree_ref[...].astype(F32))
    return jnp.broadcast_to(inv_root, (TILE, TILE)).T


def scale_out_kernel(degree_ref, grad_out_ref, weight_out_ref, out_ref):
    delta = lax.dot_general(grad_out_ref[...], weight_out_ref[...], BY_ROWS, preferred_element_type=F32)
    out_ref[...] = (column_scale(degree_ref) * delta).astype(BF16)


def spread_tiles_kernel(x_ref, source_ref, count_ref, tiles_ref, *out_refs):
    for out_ref in out_refs:
        out_ref[...] = jnp.zeros_like(out_ref)

    def step(slot, carry):
        source = source_ref[0, slot]
        line = lax.div(source, LINE)
        columns = pl.ds(pl.multiple_of((source - line * LINE) * TILE, TILE), TILE)
        away = (line - x_ref[0] + NX) & (NX - 1)
        for k, out_ref in enumerate(out_refs):

            @pl.when(away == k)
            def _():
                out_ref[:, columns] = tiles_ref[0, slot]

        return carry

    lax.fori_loop(0, count_ref[0], step, 0)


def out_parts_kernel(x_ref, t0_ref, t1_ref, t2_ref, t3_ref, blocks_ref, out_ref):
    for k, tiles_ref in enumerate((t0_ref, t1_ref, t2_ref, t3_ref)):
        part = jnp.dot(tiles_ref[...], blocks_ref[...], preferred_element_type=F32)
        out_ref[(x_ref[0] - k + NX) & (NX - 1)] = part.astype(BF16)


def hidden_kernel(
    degree_ref, got_ref, pre_hidden_ref, agg_hidden_ref, grad_out_ref, agg_input_ref, scaled_ref, weight_ref
):
    scale = column_scale(degree_ref)
    summed = (got_ref[0].astype(F32) + got_ref[1].astype(F32)) + (got_ref[2].astype(F32) + got_ref[3].astype(F32))
    grad_pre = jnp.where(pre_hidden_ref[...].astype(F32) > 0, scale * summed, 0.0).astype(BF16)
    scaled_ref[...] = (scale * grad_pre.astype(F32)).astype(BF16)
    w_out = lax.dot_general(agg_hidden_ref[...], grad_out_ref[...], ACROSS, preferred_element_type=F32)
    for j in range(8):
        weight_ref[j] = w_out[:, j * TILE : (j + 1) * TILE].astype(BF16)
    w_in = lax.dot_general(agg_input_ref[...], grad_pre, ACROSS, preferred_element_type=F32)
    for j in range(4):
        weight_ref[8 + j] = w_in[j * TILE : (j + 1) * TILE].astype(BF16)


def pre_parts_kernel(x_ref, t0_ref, t1_ref, t2_ref, t3_ref, blocks_ref, weight_ref, out_ref):
    total = weight_ref[0].astype(F32)
    for j in range(1, NZ):
        total = total + weight_ref[j].astype(F32)
    total = total.astype(BF16)
    for k, tiles_ref in enumerate((t0_ref, t1_ref, t2_ref, t3_ref)):
        part = jnp.dot(tiles_ref[...], blocks_ref[...], preferred_element_type=F32)
        out_ref[(x_ref[0] - k + NX) & (NX - 1), :TILE] = part.astype(BF16)
        out_ref[k, TILE:] = total


def spread_kernel(degree_ref, got_ref, spread_ref, weight_ref):
    total = (got_ref[0].astype(F32) + got_ref[1].astype(F32)) + (got_ref[2].astype(F32) + got_ref[3].astype(F32))
    spread = (column_scale(degree_ref) * total[:TILE]).astype(BF16)
    for j in range(NREP):
        spread_ref[j] = spread
    weight_ref[...] = total[TILE:].astype(BF16)


def final_kernel(weights_ref, spread_ref, weight_in_ref, w_out_ref, w_in_ref, input_ref):
    for j in range(8):
        w_out_ref[:, j * TILE : (j + 1) * TILE] = weights_ref[2 * j].astype(F32) + weights_ref[2 * j + 1].astype(F32)
    for j in range(4):
        w_in_ref[j * TILE : (j + 1) * TILE] = weights_ref[16 + 2 * j].astype(F32) + weights_ref[17 + 2 * j].astype(F32)
    total = jnp.zeros((TILE, 512), F32)
    for k in range(NREP):
        total = total + lax.dot_general(spread_ref[k], weight_in_ref[k], BY_ROWS, preferred_element_type=F32)
    input_ref[...] = total


def local(
    grad_out,
    agg_hidden,
    pre_hidden,
    agg_input,
    weight_in,
    weight_out,
    edge_tiles,
    tile_source,
    tile_count,
    degree,
):
    shape = jax.ShapeDtypeStruct
    block = shape((TILE, TILE), BF16)
    x = (lax.axis_index("blk") // LINE).astype(jnp.int32).reshape(1)
    degree = degree.reshape(1, TILE)

    with jax.named_scope("spread_tiles"):
        tiles = call(
            spread_tiles_kernel, [shape((TILE, WIDE), BF16)] * NX, [smem()] * 3 + [vmem()], 1000000, 5000000
        )(x, tile_source, tile_count, edge_tiles)
    with jax.named_scope("exchange_tiles"):
        tiles = [tiles[0]] + [lax.ppermute(tiles[k], "blk", along_x(k)) for k in range(1, NX)]
    with jax.named_scope("weight_in_gather"):
        weights_in = jnp.broadcast_to(weight_in[None], (NREP, 512, TILE))
        weights_in = lax.all_to_all(weights_in, "rep", 0, 0, tiled=True)
    with jax.named_scope("scale_out"):
        scaled = call(scale_out_kernel, block, [vmem()] * 3, 2 * 128 * 128 * 1024, 600000)(
            degree, grad_out, weight_out
        )
    with jax.named_scope("gather_out"):
        blocks = lax.all_gather(scaled, "blk", axis=0, tiled=True, axis_index_groups=LINE_GROUPS)
    blocks, weights_in = lax.optimization_barrier((blocks, weights_in))
    with jax.named_scope("out_parts"):
        parts = call(
            out_parts_kernel, shape((NX, TILE, TILE), BF16), [smem()] + [vmem()] * 5, 2 * 512 * 3072 * 128, 4000000
        )(x, *tiles, blocks)
    with jax.named_scope("sum_out_x"):
        parts = lax.all_to_all(parts, "blk", 0, 0, tiled=True, axis_index_groups=X_GROUPS)
    with jax.named_scope("hidden"):
        scaled, weights = call(
            hidden_kernel, [block, shape((NZ, TILE, TILE), BF16)], [vmem()] * 6, 2 * 128 * 128 * 1536, 1200000
        )(degree, parts, pre_hidden, agg_hidden, grad_out, agg_input)
    with jax.named_scope("sum_weights_z"):
        weights = lax.all_to_all(weights, "blk", 0, 0, tiled=True, axis_index_groups=Z_GROUPS)
    with jax.named_scope("gather_pre"):
        blocks = lax.all_gather(scaled, "blk", axis=0, tiled=True, axis_index_groups=LINE_GROUPS)
    with jax.named_scope("pre_parts"):
        parts = call(
            pre_parts_kernel,
            shape((NX, 2 * TILE, TILE), BF16),
            [smem()] + [vmem()] * 6,
            2 * 512 * 3072 * 128,
            4500000,
        )(x, *tiles, blocks, weights)
    with jax.named_scope("sum_pre_x"):
        parts = lax.all_to_all(parts, "blk", 0, 0, tiled=True, axis_index_groups=X_GROUPS)
    with jax.named_scope("spread"):
        spread, weights = call(
            spread_kernel, [shape((NREP, TILE, TILE), BF16), block], [vmem()] * 2, 500000, 600000
        )(degree, parts)
    with jax.named_scope("gather_spread"):
        spread = lax.all_to_all(spread, "rep", 0, 0, tiled=True)
    with jax.named_scope("gather_weights"):
        weights = lax.all_gather(weights, "blk", axis=0, tiled=False, axis_index_groups=LINE_GROUPS)
    with jax.named_scope("final"):
        return tuple(
            call(
                final_kernel,
                [shape((128, 1024), F32), shape((512, 128), F32), shape((128, 512), F32)],
                [vmem()] * 3,
                2 * 128 * 1024 * 512,
                2500000,
            )(weights, spread, weights_in)
        )


def solution(mesh):
    return jax.shard_map(
        local,
        mesh=mesh,
        in_specs=(
            P("blk", None),
            P("blk", "rep"),
            P("blk", "rep"),
            P("blk", None),
            P(None, "rep"),
            P("rep", None),
            P("blk", None, None, None),
            P("blk", None),
            P("blk"),
            P("blk"),
        ),
        out_specs=(P("rep", None), P(None, "rep"), P("blk", None)),
        check_vma=False,
    )
```

```python
import jax
import jax.numpy as jnp
from jax import lax
from jax.experimental import pallas as pl
from jax.experimental.pallas import tpu as pltpu
from jax.sharding import PartitionSpec as P

TILE = 128
NX, NZ, NC = 4, 12, 2
NREP = 8
LINE = NZ * NC
WIDE = LINE * TILE
PIECE = 24
CHUNK = NX * PIECE
ROOM = 32
BF16 = jnp.bfloat16
F32 = jnp.float32
VMEM_LIMIT = 14 * 1024 * 1024
ACROSS = (((0,), (0,)), ((), ()))
BY_ROWS = (((1,), (1,)), ((), ()))


def blk_index(x, z, c):
    return (x * NZ + z) * NC + c


Z_GROUPS = [[blk_index(x, z, c) for z in range(NZ)] for x in range(NX) for c in range(NC)]
X_GROUPS = [[blk_index(x, z, c) for x in range(NX)] for z in range(NZ) for c in range(NC)]
LINE_GROUPS = [[x * LINE + p for p in range(LINE)] for x in range(NX)]


def along_x(k):
    return [(x * LINE + p, (x + k) % NX * LINE + p) for x in range(NX) for p in range(LINE)]


def vmem():
    return pl.BlockSpec(memory_space=pltpu.VMEM)


def smem():
    return pl.BlockSpec(memory_space=pltpu.SMEM)


def call(kernel, out_shape, in_specs, flops, moved):
    return pl.pallas_call(
        kernel,
        out_shape=out_shape,
        in_specs=in_specs,
        out_specs=jax.tree.map(lambda _: vmem(), out_shape),
        compiler_params=pltpu.CompilerParams(vmem_limit_bytes=VMEM_LIMIT),
        cost_estimate=pl.CostEstimate(flops=flops, bytes_accessed=moved, transcendentals=0),
    )


def column_scale(degree_ref):
    inv_root = 1.0 / jnp.sqrt(degree_ref[...].astype(F32))
    return jnp.broadcast_to(inv_root, (TILE, TILE)).T


def scale_out_kernel(degree_ref, grad_out_ref, weight_out_ref, agg_hidden_ref, scaled_ref, weight_ref):
    delta = lax.dot_general(grad_out_ref[...], weight_out_ref[...], BY_ROWS, preferred_element_type=F32)
    scaled_ref[...] = (column_scale(degree_ref) * delta).astype(BF16)
    w_out = lax.dot_general(agg_hidden_ref[...], grad_out_ref[...], ACROSS, preferred_element_type=F32)
    for j in range(8):
        weight_ref[j * TILE : (j + 1) * TILE] = w_out[:, j * TILE : (j + 1) * TILE].astype(BF16)
    weight_ref[8 * TILE :] = jnp.zeros((NZ * CHUNK - 8 * TILE, TILE), BF16)


def turn_input_kernel(degree_ref, agg_input_ref, out_ref):
    root = jnp.sqrt(degree_ref[...].astype(F32))
    for j in range(4):
        rows = slice(j * TILE, (j + 1) * TILE)
        out_ref[rows] = (agg_input_ref[:, rows].astype(F32).T * root).astype(BF16)


def spread_tiles_kernel(x_ref, source_ref, count_ref, tiles_ref, *out_refs):
    for out_ref in out_refs:
        out_ref[...] = jnp.zeros_like(out_ref)

    def step(slot, carry):
        source = source_ref[0, slot]
        line = lax.div(source, LINE)
        columns = pl.ds(pl.multiple_of((source - line * LINE) * TILE, TILE), TILE)
        away = (line - x_ref[0] + NX) & (NX - 1)
        for k, out_ref in enumerate(out_refs):

            @pl.when(away == k)
            def _():
                out_ref[:, columns] = tiles_ref[0, slot]

        return carry

    lax.fori_loop(0, count_ref[0], step, 0)


def multiply(tiles_refs, blocks):
    return [jnp.dot(tiles_ref[...], blocks, preferred_element_type=F32).astype(BF16) for tiles_ref in tiles_refs]


def out_parts_kernel(x_ref, t0_ref, t1_ref, t2_ref, t3_ref, blocks_ref, weight_ref, out_ref):
    parts = multiply((t0_ref, t1_ref, t2_ref, t3_ref), blocks_ref[...])
    total = weight_ref[0].astype(F32)
    for j in range(1, NZ):
        total = total + weight_ref[j].astype(F32)
    for k in range(NX):
        out_ref[(x_ref[0] - k + NX) & (NX - 1), :TILE] = parts[k]
        piece = total[k * PIECE : (k + 1) * PIECE]
        piece = jnp.concatenate([piece, jnp.zeros((ROOM - PIECE, TILE), F32)], axis=0)
        out_ref[k, TILE:] = piece.astype(BF16)


def sum_lines(got_ref):
    return (got_ref[0].astype(F32) + got_ref[1].astype(F32)) + (got_ref[2].astype(F32) + got_ref[3].astype(F32))


def hidden_kernel(degree_ref, got_ref, pre_hidden_ref, out_ref):
    scale = column_scale(degree_ref)
    total = sum_lines(got_ref)
    grad_pre = jnp.where(pre_hidden_ref[...].astype(F32) > 0, scale * total[:TILE], 0.0).astype(BF16)
    out_ref[:TILE] = (scale * grad_pre.astype(F32)).astype(BF16)
    out_ref[TILE:] = total[TILE:].astype(BF16)


def pre_parts_kernel(x_ref, t0_ref, t1_ref, t2_ref, t3_ref, blocks_ref, turned_ref, out_ref, weight_ref):
    blocks = blocks_ref[:, :TILE].reshape(WIDE, TILE)
    parts = multiply((t0_ref, t1_ref, t2_ref, t3_ref), blocks)
    w_in = jnp.zeros((4 * TILE, TILE), F32)
    for p in range(0, LINE, 2):
        turned = jnp.concatenate([turned_ref[p], turned_ref[p + 1]], axis=1)
        w_in = w_in + jnp.dot(turned, blocks[p * TILE : (p + 2) * TILE], preferred_element_type=F32)
    for k in range(NX):
        out_ref[(x_ref[0] - k + NX) & (NX - 1), :TILE] = parts[k]
        out_ref[k, TILE:] = w_in[k * TILE : (k + 1) * TILE].astype(BF16)
    pieces = []
    for z in range(NZ):
        both = blocks_ref[2 * z, TILE:].astype(F32) + blocks_ref[2 * z + 1, TILE:].astype(F32)
        pieces.append(both[:PIECE])
    weight_ref[...] = jnp.concatenate(pieces, axis=0).astype(BF16)


def spread_kernel(degree_ref, got_ref, w_out_ref, spread_ref, weight_ref):
    total = sum_lines(got_ref)
    spread = (column_scale(degree_ref) * total[:TILE]).astype(BF16)
    for j in range(NREP):
        spread_ref[j] = spread
    weight_ref[: NZ * PIECE] = w_out_ref[...]
    weight_ref[NZ * PIECE :] = total[TILE:].astype(BF16)


def final_kernel(weights_ref, spread_ref, weight_in_ref, w_out_ref, w_in_ref, input_ref):
    for x in range(NX):
        weights = weights_ref[x].astype(F32)
        for z in range(NZ):
            row = z * CHUNK + x * PIECE
            at, left = z * PIECE, min(PIECE, 8 * TILE - row)
            while left > 0:
                j, r = row // TILE, row % TILE
                n = min(left, TILE - r)
                w_out_ref[r : r + n, j * TILE : (j + 1) * TILE] = weights[at : at + n]
                row, at, left = row + n, at + n, left - n
        w_in_ref[x * TILE : (x + 1) * TILE] = weights[NZ * PIECE :]
    total = jnp.zeros((TILE, 512), F32)
    for k in range(NREP):
        total = total + lax.dot_general(spread_ref[k], weight_in_ref[k], BY_ROWS, preferred_element_type=F32)
    input_ref[...] = total


def local(
    grad_out,
    agg_hidden,
    pre_hidden,
    agg_input,
    weight_in,
    weight_out,
    edge_tiles,
    tile_source,
    tile_count,
    degree,
):
    shape = jax.ShapeDtypeStruct
    block = shape((TILE, TILE), BF16)
    x = (lax.axis_index("blk") // LINE).astype(jnp.int32).reshape(1)
    degree = degree.reshape(1, TILE)

    with jax.named_scope("turn_input"):
        turned = call(turn_input_kernel, shape((4 * TILE, TILE), BF16), [vmem()] * 2, 300000, 300000)(degree, agg_input)
    with jax.named_scope("gather_input"):
        turned = lax.all_gather(turned, "blk", axis=0, tiled=False, axis_index_groups=LINE_GROUPS)
    with jax.named_scope("gather_weight_in"):
        weights_in = lax.all_gather(weight_in, "rep", axis=0, tiled=False)
    with jax.named_scope("spread_tiles"):
        tiles = call(
            spread_tiles_kernel, [shape((TILE, WIDE), BF16)] * NX, [smem()] * 3 + [vmem()], 1000000, 5000000
        )(x, tile_source, tile_count, edge_tiles)
    with jax.named_scope("exchange_tiles"):
        tiles = [tiles[0]] + [lax.ppermute(tiles[k], "blk", along_x(k)) for k in range(1, NX)]
    with jax.named_scope("scale_out"):
        scaled, weights = call(
            scale_out_kernel, [block, shape((NZ * CHUNK, TILE), BF16)], [vmem()] * 4, 4 * 128 * 128 * 1024, 900000
        )(degree, grad_out, weight_out, agg_hidden)
    with jax.named_scope("sum_weights_z"):
        weights = weights.reshape(NZ, CHUNK, TILE)
        weights = lax.all_to_all(weights, "blk", 0, 0, tiled=True, axis_index_groups=Z_GROUPS)
    with jax.named_scope("gather_out"):
        blocks = lax.all_gather(scaled, "blk", axis=0, tiled=True, axis_index_groups=LINE_GROUPS)
    with jax.named_scope("out_parts"):
        parts = call(
            out_parts_kernel,
            shape((NX, TILE + ROOM, TILE), BF16),
            [smem()] + [vmem()] * 6,
            2 * 512 * 3072 * 128,
            4000000,
        )(x, *tiles, blocks, weights)
    with jax.named_scope("sum_out_x"):
        parts = lax.all_to_all(parts, "blk", 0, 0, tiled=True, axis_index_groups=X_GROUPS)
    with jax.named_scope("hidden"):
        scaled = call(hidden_kernel, shape((TILE + ROOM, TILE), BF16), [vmem()] * 3, 1000000, 600000)(
            degree, parts, pre_hidden
        )
    with jax.named_scope("gather_pre"):
        blocks = lax.all_gather(scaled, "blk", axis=0, tiled=False, axis_index_groups=LINE_GROUPS)
    with jax.named_scope("pre_parts"):
        parts, w_out = call(
            pre_parts_kernel,
            [shape((NX, 2 * TILE, TILE), BF16), shape((NZ * PIECE, TILE), BF16)],
            [smem()] + [vmem()] * 6,
            4 * 512 * 3072 * 128,
            8000000,
        )(x, *tiles, blocks, turned)
    with jax.named_scope("sum_pre_x"):
        parts = lax.all_to_all(parts, "blk", 0, 0, tiled=True, axis_index_groups=X_GROUPS)
    parts, weights_in = lax.optimization_barrier((parts, weights_in))
    with jax.named_scope("spread"):
        spread, weights = call(
            spread_kernel,
            [shape((NREP, TILE, TILE), BF16), shape((NZ * PIECE + TILE, TILE), BF16)],
            [vmem()] * 3,
            500000,
            800000,
        )(degree, parts, w_out)
    with jax.named_scope("gather_spread"):
        spread = lax.all_to_all(spread, "rep", 0, 0, tiled=True)
    with jax.named_scope("gather_weights"):
        weights = lax.all_gather(weights, "blk", axis=0, tiled=False, axis_index_groups=X_GROUPS)
    with jax.named_scope("final"):
        return tuple(
            call(
                final_kernel,
                [shape((128, 1024), F32), shape((512, 128), F32), shape((128, 512), F32)],
                [vmem()] * 3,
                2 * 128 * 1024 * 512,
                2500000,
            )(weights, spread, weights_in)
        )


def solution(mesh):
    return jax.shard_map(
        local,
        mesh=mesh,
        in_specs=(
            P("blk", None),
            P("blk", "rep"),
            P("blk", "rep"),
            P("blk", None),
            P(None, "rep"),
            P("rep", None),
            P("blk", None, None, None),
            P("blk", None),
            P("blk"),
            P("blk"),
        ),
        out_specs=(P("rep", None), P(None, "rep"), P("blk", None)),
        check_vma=False,
    )
```

```python
import jax
import jax.numpy as jnp
from jax import lax
from jax.experimental import pallas as pl
from jax.experimental.pallas import tpu as pltpu
from jax.sharding import PartitionSpec as P

TILE = 128
NX, NZ, NC = 4, 12, 2
NREP = 8
LINE = NZ * NC
WIDE = LINE * TILE
PIECE = 24
CHUNK = NX * PIECE
ROOM = 32
BF16 = jnp.bfloat16
F32 = jnp.float32
MIB = 1024 * 1024
ACROSS = (((0,), (0,)), ((), ()))
BY_ROWS = (((1,), (1,)), ((), ()))


def blk_index(x, z, c):
    return (x * NZ + z) * NC + c


Z_GROUPS = [[blk_index(x, z, c) for z in range(NZ)] for x in range(NX) for c in range(NC)]
X_GROUPS = [[blk_index(x, z, c) for x in range(NX)] for z in range(NZ) for c in range(NC)]
LINE_GROUPS = [[x * LINE + p for p in range(LINE)] for x in range(NX)]


def along_x(k):
    return [(x * LINE + p, (x + k) % NX * LINE + p) for x in range(NX) for p in range(LINE)]


def vmem():
    return pl.BlockSpec(memory_space=pltpu.VMEM)


def smem():
    return pl.BlockSpec(memory_space=pltpu.SMEM)


def hbm():
    return pl.BlockSpec(memory_space=pltpu.HBM)


def call(kernel, out_shape, in_specs, flops, moved, scratch=(), limit=14):
    return pl.pallas_call(
        kernel,
        out_shape=out_shape,
        in_specs=in_specs,
        out_specs=jax.tree.map(lambda _: vmem(), out_shape),
        scratch_shapes=scratch,
        compiler_params=pltpu.CompilerParams(vmem_limit_bytes=limit * MIB),
        cost_estimate=pl.CostEstimate(flops=flops, bytes_accessed=moved, transcendentals=0),
    )


def column_scale(degree_ref):
    inv_root = 1.0 / jnp.sqrt(degree_ref[...].astype(F32))
    return jnp.broadcast_to(inv_root, (TILE, TILE)).T


def start_kernel(
    x_ref,
    count_ref,
    source_hbm,
    degree_hbm,
    grad_out_hbm,
    weight_out_hbm,
    agg_hidden_hbm,
    agg_input_hbm,
    tiles_hbm,
    t0_ref,
    t1_ref,
    t2_ref,
    t3_ref,
    scaled_ref,
    weight_ref,
    turned_ref,
    source_ref,
    degree_ref,
    grad_out_ref,
    weight_out_ref,
    agg_hidden_ref,
    agg_input_ref,
    tiles_ref,
    sems,
):
    pairs = (
        (source_hbm, source_ref),
        (tiles_hbm, tiles_ref),
        (degree_hbm, degree_ref),
        (agg_input_hbm, agg_input_ref),
        (grad_out_hbm, grad_out_ref),
        (weight_out_hbm, weight_out_ref),
        (agg_hidden_hbm, agg_hidden_ref),
    )
    copies = [pltpu.make_async_copy(there, here, sems.at[i]) for i, (there, here) in enumerate(pairs)]
    for copy in copies:
        copy.start()
    out_refs = (t0_ref, t1_ref, t2_ref, t3_ref)
    for out_ref in out_refs:
        out_ref[...] = jnp.zeros_like(out_ref)
    weight_ref[8 * TILE :] = jnp.zeros((NZ * CHUNK - 8 * TILE, TILE), BF16)
    for copy in copies:
        copy.wait()

    root = jnp.sqrt(degree_ref[...].astype(F32))
    for j in range(4):
        rows = slice(j * TILE, (j + 1) * TILE)
        turned_ref[rows] = (agg_input_ref[:, rows].astype(F32).T * root).astype(BF16)

    def step(slot, carry):
        source = source_ref[0, slot]
        line = lax.div(source, LINE)
        columns = pl.ds(pl.multiple_of((source - line * LINE) * TILE, TILE), TILE)
        away = (line - x_ref[0] + NX) & (NX - 1)
        for k, out_ref in enumerate(out_refs):

            @pl.when(away == k)
            def _():
                out_ref[:, columns] = tiles_ref[0, slot]

        return carry

    lax.fori_loop(0, count_ref[0], step, 0)
    delta = lax.dot_general(grad_out_ref[...], weight_out_ref[...], BY_ROWS, preferred_element_type=F32)
    scaled_ref[...] = (column_scale(degree_ref) * delta).astype(BF16)
    w_out = lax.dot_general(agg_hidden_ref[...], grad_out_ref[...], ACROSS, preferred_element_type=F32)
    for j in range(8):
        weight_ref[j * TILE : (j + 1) * TILE] = w_out[:, j * TILE : (j + 1) * TILE].astype(BF16)


def multiply(tiles_refs, blocks):
    return [jnp.dot(tiles_ref[...], blocks, preferred_element_type=F32).astype(BF16) for tiles_ref in tiles_refs]


def out_parts_kernel(x_ref, t0_ref, t1_ref, t2_ref, t3_ref, blocks_ref, weight_ref, out_ref):
    parts = multiply((t0_ref, t1_ref, t2_ref, t3_ref), blocks_ref[...])
    total = weight_ref[0].astype(F32)
    for j in range(1, NZ):
        total = total + weight_ref[j].astype(F32)
    for k in range(NX):
        out_ref[(x_ref[0] - k + NX) & (NX - 1), :TILE] = parts[k]
        piece = total[k * PIECE : (k + 1) * PIECE]
        piece = jnp.concatenate([piece, jnp.zeros((ROOM - PIECE, TILE), F32)], axis=0)
        out_ref[k, TILE:] = piece.astype(BF16)


def sum_lines(got_ref):
    return (got_ref[0].astype(F32) + got_ref[1].astype(F32)) + (got_ref[2].astype(F32) + got_ref[3].astype(F32))


def hidden_kernel(degree_ref, got_ref, pre_hidden_ref, out_ref):
    scale = column_scale(degree_ref)
    total = sum_lines(got_ref)
    grad_pre = jnp.where(pre_hidden_ref[...].astype(F32) > 0, scale * total[:TILE], 0.0).astype(BF16)
    out_ref[:TILE] = (scale * grad_pre.astype(F32)).astype(BF16)
    out_ref[TILE:] = total[TILE:].astype(BF16)


def pre_parts_kernel(
    x_ref, t0_ref, t1_ref, t2_ref, t3_ref, blocks_ref, turned_hbm, out_ref, weight_ref, turned_ref, sem
):
    copy = pltpu.make_async_copy(turned_hbm, turned_ref, sem)
    copy.start()
    blocks = blocks_ref[:, :TILE].reshape(WIDE, TILE)
    parts = multiply((t0_ref, t1_ref, t2_ref, t3_ref), blocks)
    for k in range(NX):
        out_ref[(x_ref[0] - k + NX) & (NX - 1), :TILE] = parts[k]
    pieces = []
    for z in range(NZ):
        both = blocks_ref[2 * z, TILE:].astype(F32) + blocks_ref[2 * z + 1, TILE:].astype(F32)
        pieces.append(both[:PIECE])
    weight_ref[...] = jnp.concatenate(pieces, axis=0).astype(BF16)
    copy.wait()
    w_in = jnp.zeros((4 * TILE, TILE), F32)
    for p in range(0, LINE, 2):
        turned = jnp.concatenate([turned_ref[p], turned_ref[p + 1]], axis=1)
        w_in = w_in + jnp.dot(turned, blocks[p * TILE : (p + 2) * TILE], preferred_element_type=F32)
    for k in range(NX):
        out_ref[k, TILE:] = w_in[k * TILE : (k + 1) * TILE].astype(BF16)


def spread_kernel(degree_ref, got_ref, w_out_ref, spread_ref, weight_ref):
    total = sum_lines(got_ref)
    spread = (column_scale(degree_ref) * total[:TILE]).astype(BF16)
    for j in range(NREP):
        spread_ref[j] = spread
    weight_ref[: NZ * PIECE] = w_out_ref[...]
    weight_ref[NZ * PIECE :] = total[TILE:].astype(BF16)


def final_kernel(weights_ref, spread_ref, weight_in_hbm, w_out_ref, w_in_ref, input_ref, weight_in_ref, sem):
    copy = pltpu.make_async_copy(weight_in_hbm, weight_in_ref, sem)
    copy.start()
    for x in range(NX):
        weights = weights_ref[x].astype(F32)
        for z in range(NZ):
            row = z * CHUNK + x * PIECE
            at, left = z * PIECE, min(PIECE, 8 * TILE - row)
            while left > 0:
                j, r = row // TILE, row % TILE
                n = min(left, TILE - r)
                w_out_ref[r : r + n, j * TILE : (j + 1) * TILE] = weights[at : at + n]
                row, at, left = row + n, at + n, left - n
        w_in_ref[x * TILE : (x + 1) * TILE] = weights[NZ * PIECE :]
    copy.wait()
    total = jnp.zeros((TILE, 512), F32)
    for k in range(NREP):
        total = total + lax.dot_general(spread_ref[k], weight_in_ref[k], BY_ROWS, preferred_element_type=F32)
    input_ref[...] = total


def local(
    grad_out,
    agg_hidden,
    pre_hidden,
    agg_input,
    weight_in,
    weight_out,
    edge_tiles,
    tile_source,
    tile_count,
    degree,
):
    shape = jax.ShapeDtypeStruct
    block = shape((TILE, TILE), BF16)
    x = (lax.axis_index("blk") // LINE).astype(jnp.int32).reshape(1)
    degree = degree.reshape(1, TILE)

    copied = [tile_source, degree, grad_out, weight_out, agg_hidden, agg_input, edge_tiles]
    homes = [pltpu.SMEM] + [pltpu.VMEM] * 6
    with jax.named_scope("start"):
        *tiles, scaled, weights, turned = call(
            start_kernel,
            [shape((TILE, WIDE), BF16)] * NX
            + [block, shape((NZ * CHUNK, TILE), BF16), shape((4 * TILE, TILE), BF16)],
            [smem()] * 2 + [hbm()] * 7,
            4 * 128 * 128 * 1024,
            6000000,
            [home(a.shape, a.dtype) for home, a in zip(homes, copied)] + [pltpu.SemaphoreType.DMA((7,))],
            limit=56,
        )(x, tile_count, *copied)
    with jax.named_scope("gather_input"):
        turned = lax.all_gather(turned, "blk", axis=0, tiled=False, axis_index_groups=LINE_GROUPS)
    with jax.named_scope("gather_weight_in"):
        weights_in = lax.all_gather(weight_in, "rep", axis=0, tiled=False)
    with jax.named_scope("exchange_tiles"):
        tiles = [tiles[0]] + [lax.ppermute(tiles[k], "blk", along_x(k)) for k in range(1, NX)]
    with jax.named_scope("sum_weights_z"):
        weights = weights.reshape(NZ, CHUNK, TILE)
        weights = lax.all_to_all(weights, "blk", 0, 0, tiled=True, axis_index_groups=Z_GROUPS)
    with jax.named_scope("gather_out"):
        blocks = lax.all_gather(scaled, "blk", axis=0, tiled=True, axis_index_groups=LINE_GROUPS)
    with jax.named_scope("out_parts"):
        parts = call(
            out_parts_kernel,
            shape((NX, TILE + ROOM, TILE), BF16),
            [smem()] + [vmem()] * 6,
            2 * 512 * 3072 * 128,
            4000000,
            limit=50,
        )(x, *tiles, blocks, weights)
    with jax.named_scope("sum_out_x"):
        parts = lax.all_to_all(parts, "blk", 0, 0, tiled=True, axis_index_groups=X_GROUPS)
    with jax.named_scope("hidden"):
        scaled = call(hidden_kernel, shape((TILE + ROOM, TILE), BF16), [vmem()] * 3, 1000000, 600000)(
            degree, parts, pre_hidden
        )
    with jax.named_scope("gather_pre"):
        blocks = lax.all_gather(scaled, "blk", axis=0, tiled=False, axis_index_groups=LINE_GROUPS)
    with jax.named_scope("pre_parts"):
        parts, w_out = call(
            pre_parts_kernel,
            [shape((NX, 2 * TILE, TILE), BF16), shape((NZ * PIECE, TILE), BF16)],
            [smem()] + [vmem()] * 5 + [hbm()],
            4 * 512 * 3072 * 128,
            8000000,
            [pltpu.VMEM((LINE, 4 * TILE, TILE), BF16), pltpu.SemaphoreType.DMA],
            limit=50,
        )(x, *tiles, blocks, turned)
    with jax.named_scope("sum_pre_x"):
        parts = lax.all_to_all(parts, "blk", 0, 0, tiled=True, axis_index_groups=X_GROUPS)
    with jax.named_scope("spread"):
        spread, weights = call(
            spread_kernel,
            [shape((NREP, TILE, TILE), BF16), shape((NZ * PIECE + TILE, TILE), BF16)],
            [vmem()] * 3,
            500000,
            800000,
        )(degree, parts, w_out)
    with jax.named_scope("gather_spread"):
        spread = lax.all_to_all(spread, "rep", 0, 0, tiled=True)
    with jax.named_scope("gather_weights"):
        weights = lax.all_gather(weights, "blk", axis=0, tiled=False, axis_index_groups=X_GROUPS)
    with jax.named_scope("final"):
        return tuple(
            call(
                final_kernel,
                [shape((128, 1024), F32), shape((512, 128), F32), shape((128, 512), F32)],
                [vmem()] * 2 + [hbm()],
                2 * 128 * 1024 * 512,
                2500000,
                [pltpu.VMEM((NREP, 4 * TILE, TILE), BF16), pltpu.SemaphoreType.DMA],
                limit=56,
            )(weights, spread, weights_in)
        )


def solution(mesh):
    return jax.shard_map(
        local,
        mesh=mesh,
        in_specs=(
            P("blk", None),
            P("blk", "rep"),
            P("blk", "rep"),
            P("blk", None),
            P(None, "rep"),
            P("rep", None),
            P("blk", None, None, None),
            P("blk", None),
            P("blk"),
            P("blk"),
        ),
        out_specs=(P("rep", None), P(None, "rep"), P("blk", None)),
        check_vma=False,
    )
```

```python
import jax
import jax.numpy as jnp
from jax import lax
from jax.experimental import pallas as pl
from jax.experimental.pallas import tpu as pltpu
from jax.sharding import PartitionSpec as P

TILE = 128
NX, NZ, NC = 4, 12, 2
NREP = 8
LINE = NZ * NC
WIDE = LINE * TILE
PIECE = 24
CHUNK = NX * PIECE
ROOM = 32
BF16 = jnp.bfloat16
F32 = jnp.float32
MIB = 1024 * 1024
ACROSS = (((0,), (0,)), ((), ()))
BY_ROWS = (((1,), (1,)), ((), ()))


def blk_index(x, z, c):
    return (x * NZ + z) * NC + c


Z_GROUPS = [[blk_index(x, z, c) for z in range(NZ)] for x in range(NX) for c in range(NC)]
X_GROUPS = [[blk_index(x, z, c) for x in range(NX)] for z in range(NZ) for c in range(NC)]
LINE_GROUPS = [[x * LINE + p for p in range(LINE)] for x in range(NX)]


def along_x(k):
    return [(x * LINE + p, (x + k) % NX * LINE + p) for x in range(NX) for p in range(LINE)]


def vmem():
    return pl.BlockSpec(memory_space=pltpu.VMEM)


def smem():
    return pl.BlockSpec(memory_space=pltpu.SMEM)


def hbm():
    return pl.BlockSpec(memory_space=pltpu.HBM)


def call(kernel, out_shape, in_specs, flops, moved, scratch=(), limit=14):
    return pl.pallas_call(
        kernel,
        out_shape=out_shape,
        in_specs=in_specs,
        out_specs=jax.tree.map(lambda _: vmem(), out_shape),
        scratch_shapes=scratch,
        compiler_params=pltpu.CompilerParams(vmem_limit_bytes=limit * MIB),
        cost_estimate=pl.CostEstimate(flops=flops, bytes_accessed=moved, transcendentals=0),
    )


def column_scale(degree_ref):
    inv_root = 1.0 / jnp.sqrt(degree_ref[...].astype(F32))
    return jnp.broadcast_to(inv_root, (TILE, TILE)).T


def start_kernel(
    x_ref,
    count_ref,
    source_hbm,
    degree_hbm,
    grad_out_hbm,
    weight_out_hbm,
    agg_hidden_hbm,
    agg_input_hbm,
    tiles_hbm,
    t0_ref,
    t1_ref,
    t2_ref,
    t3_ref,
    scaled_ref,
    weight_ref,
    turned_ref,
    source_ref,
    degree_ref,
    grad_out_ref,
    weight_out_ref,
    agg_hidden_ref,
    agg_input_ref,
    tiles_ref,
    sems,
):
    pairs = (
        (source_hbm, source_ref),
        (tiles_hbm, tiles_ref),
        (degree_hbm, degree_ref),
        (agg_input_hbm, agg_input_ref),
        (grad_out_hbm, grad_out_ref),
        (weight_out_hbm, weight_out_ref),
        (agg_hidden_hbm, agg_hidden_ref),
    )
    copies = [pltpu.make_async_copy(there, here, sems.at[i]) for i, (there, here) in enumerate(pairs)]
    for copy in copies:
        copy.start()
    out_refs = (t0_ref, t1_ref, t2_ref, t3_ref)
    for out_ref in out_refs:
        out_ref[...] = jnp.zeros_like(out_ref)
    weight_ref[8 * TILE :] = jnp.zeros((NZ * CHUNK - 8 * TILE, TILE), BF16)
    for copy in copies:
        copy.wait()

    root = jnp.sqrt(degree_ref[...].astype(F32))
    for j in range(4):
        rows = slice(j * TILE, (j + 1) * TILE)
        turned_ref[rows] = (agg_input_ref[:, rows].astype(F32).T * root).astype(BF16)

    def step(slot, carry):
        source = source_ref[0, slot]
        line = lax.div(source, LINE)
        columns = pl.ds(pl.multiple_of((source - line * LINE) * TILE, TILE), TILE)
        away = (line - x_ref[0] + NX) & (NX - 1)
        for k, out_ref in enumerate(out_refs):

            @pl.when(away == k)
            def _():
                out_ref[:, columns] = tiles_ref[0, slot]

        return carry

    lax.fori_loop(0, count_ref[0], step, 0)
    delta = lax.dot_general(grad_out_ref[...], weight_out_ref[...], BY_ROWS, preferred_element_type=F32)
    scaled_ref[...] = (column_scale(degree_ref) * delta).astype(BF16)
    w_out = lax.dot_general(agg_hidden_ref[...], grad_out_ref[...], ACROSS, preferred_element_type=F32)
    for j in range(8):
        weight_ref[j * TILE : (j + 1) * TILE] = w_out[:, j * TILE : (j + 1) * TILE].astype(BF16)


def copy_in(pairs, parts, sems):
    started, at = [], 0
    for there, here in pairs:
        n = here.shape[0] // parts
        copies = []
        for i in range(parts):
            rows = pl.ds(i * n, n)
            copies.append(pltpu.make_async_copy(there.at[rows], here.at[rows], sems.at[at]))
            copies[-1].start()
            at += 1
        started.append(copies)
    return started


def multiply(tiles_refs, blocks):
    return [jnp.dot(tiles_ref[...], blocks, preferred_element_type=F32).astype(BF16) for tiles_ref in tiles_refs]


def out_parts_kernel(
    x_ref, t0_hbm, t1_ref, t2_ref, t3_ref, blocks_hbm, weight_ref, out_ref, blocks_ref, t0_ref, sems
):
    got, first = copy_in(((blocks_hbm, blocks_ref), (t0_hbm, t0_ref)), 4, sems)
    total = weight_ref[0].astype(F32)
    for j in range(1, NZ):
        total = total + weight_ref[j].astype(F32)
    for k in range(NX):
        piece = total[k * PIECE : (k + 1) * PIECE]
        piece = jnp.concatenate([piece, jnp.zeros((ROOM - PIECE, TILE), F32)], axis=0)
        out_ref[k, TILE:] = piece.astype(BF16)
    for copy in got + first:
        copy.wait()
    parts = multiply((t0_ref, t1_ref, t2_ref, t3_ref), blocks_ref[...])
    for k in range(NX):
        out_ref[(x_ref[0] - k + NX) & (NX - 1), :TILE] = parts[k]


def sum_lines(got_ref):
    return (got_ref[0].astype(F32) + got_ref[1].astype(F32)) + (got_ref[2].astype(F32) + got_ref[3].astype(F32))


def hidden_kernel(degree_ref, got_ref, pre_hidden_ref, out_ref):
    scale = column_scale(degree_ref)
    total = sum_lines(got_ref)
    grad_pre = jnp.where(pre_hidden_ref[...].astype(F32) > 0, scale * total[:TILE], 0.0).astype(BF16)
    out_ref[:TILE] = (scale * grad_pre.astype(F32)).astype(BF16)
    out_ref[TILE:] = total[TILE:].astype(BF16)


def pre_parts_kernel(
    x_ref,
    t0_ref,
    t1_ref,
    t2_ref,
    t3_ref,
    blocks_hbm,
    turned_hbm,
    out_ref,
    weight_ref,
    blocks_ref,
    turned_ref,
    sems,
):
    got, turned_parts = copy_in(((blocks_hbm, blocks_ref), (turned_hbm, turned_ref)), 6, sems)
    for copy in got:
        copy.wait()
    blocks = blocks_ref[:, :TILE].reshape(WIDE, TILE)
    parts = multiply((t0_ref, t1_ref, t2_ref, t3_ref), blocks)
    for k in range(NX):
        out_ref[(x_ref[0] - k + NX) & (NX - 1), :TILE] = parts[k]
    pieces = []
    for z in range(NZ):
        both = blocks_ref[2 * z, TILE:].astype(F32) + blocks_ref[2 * z + 1, TILE:].astype(F32)
        pieces.append(both[:PIECE])
    weight_ref[...] = jnp.concatenate(pieces, axis=0).astype(BF16)
    w_in = jnp.zeros((4 * TILE, TILE), F32)
    for p in range(0, LINE, 4):
        turned_parts[p // 4].wait()
        turned = jnp.concatenate([turned_ref[p + i] for i in range(4)], axis=1)
        w_in = w_in + jnp.dot(turned, blocks[p * TILE : (p + 4) * TILE], preferred_element_type=F32)
    for k in range(NX):
        out_ref[k, TILE:] = w_in[k * TILE : (k + 1) * TILE].astype(BF16)


def spread_kernel(degree_ref, got_ref, w_out_ref, spread_ref, weight_ref):
    total = sum_lines(got_ref)
    spread = (column_scale(degree_ref) * total[:TILE]).astype(BF16)
    for j in range(NREP):
        spread_ref[j] = spread
    weight_ref[: NZ * PIECE] = w_out_ref[...]
    weight_ref[NZ * PIECE :] = total[TILE:].astype(BF16)


def final_kernel(weights_ref, spread_ref, weight_in_hbm, w_out_ref, w_in_ref, input_ref, weight_in_ref, sems):
    (parts,) = copy_in(((weight_in_hbm, weight_in_ref),), NREP, sems)
    for x in range(NX):
        weights = weights_ref[x].astype(F32)
        for z in range(NZ):
            row = z * CHUNK + x * PIECE
            at, left = z * PIECE, min(PIECE, 8 * TILE - row)
            while left > 0:
                j, r = row // TILE, row % TILE
                n = min(left, TILE - r)
                w_out_ref[r : r + n, j * TILE : (j + 1) * TILE] = weights[at : at + n]
                row, at, left = row + n, at + n, left - n
        w_in_ref[x * TILE : (x + 1) * TILE] = weights[NZ * PIECE :]
    total = jnp.zeros((TILE, 512), F32)
    for k in range(NREP):
        parts[k].wait()
        total = total + lax.dot_general(spread_ref[k], weight_in_ref[k], BY_ROWS, preferred_element_type=F32)
    input_ref[...] = total


def local(
    grad_out,
    agg_hidden,
    pre_hidden,
    agg_input,
    weight_in,
    weight_out,
    edge_tiles,
    tile_source,
    tile_count,
    degree,
):
    shape = jax.ShapeDtypeStruct
    block = shape((TILE, TILE), BF16)
    x = (lax.axis_index("blk") // LINE).astype(jnp.int32).reshape(1)
    degree = degree.reshape(1, TILE)

    copied = [tile_source, degree, grad_out, weight_out, agg_hidden, agg_input, edge_tiles]
    homes = [pltpu.SMEM] + [pltpu.VMEM] * 6
    with jax.named_scope("start"):
        *tiles, scaled, weights, turned = call(
            start_kernel,
            [shape((TILE, WIDE), BF16)] * NX
            + [block, shape((NZ * CHUNK, TILE), BF16), shape((4 * TILE, TILE), BF16)],
            [smem()] * 2 + [hbm()] * 7,
            4 * 128 * 128 * 1024,
            6000000,
            [home(a.shape, a.dtype) for home, a in zip(homes, copied)] + [pltpu.SemaphoreType.DMA((7,))],
            limit=56,
        )(x, tile_count, *copied)
    with jax.named_scope("gather_input"):
        turned = lax.all_gather(turned, "blk", axis=0, tiled=False, axis_index_groups=LINE_GROUPS)
    with jax.named_scope("gather_weight_in"):
        weights_in = lax.all_gather(weight_in, "rep", axis=0, tiled=False)
    with jax.named_scope("exchange_tiles"):
        tiles = [tiles[0]] + [lax.ppermute(tiles[k], "blk", along_x(k)) for k in range(1, NX)]
    with jax.named_scope("sum_weights_z"):
        weights = weights.reshape(NZ, CHUNK, TILE)
        weights = lax.all_to_all(weights, "blk", 0, 0, tiled=True, axis_index_groups=Z_GROUPS)
    with jax.named_scope("gather_out"):
        blocks = lax.all_gather(scaled, "blk", axis=0, tiled=True, axis_index_groups=LINE_GROUPS)
    with jax.named_scope("out_parts"):
        parts = call(
            out_parts_kernel,
            shape((NX, TILE + ROOM, TILE), BF16),
            [smem(), hbm()] + [vmem()] * 3 + [hbm(), vmem()],
            2 * 512 * 3072 * 128,
            4000000,
            [pltpu.VMEM((WIDE, TILE), BF16), pltpu.VMEM((TILE, WIDE), BF16), pltpu.SemaphoreType.DMA((8,))],
            limit=50,
        )(x, *tiles, blocks, weights)
    with jax.named_scope("sum_out_x"):
        parts = lax.all_to_all(parts, "blk", 0, 0, tiled=True, axis_index_groups=X_GROUPS)
    with jax.named_scope("hidden"):
        scaled = call(hidden_kernel, shape((TILE + ROOM, TILE), BF16), [vmem()] * 3, 1000000, 600000)(
            degree, parts, pre_hidden
        )
    with jax.named_scope("gather_pre"):
        blocks = lax.all_gather(scaled, "blk", axis=0, tiled=False, axis_index_groups=LINE_GROUPS)
    with jax.named_scope("pre_parts"):
        parts, w_out = call(
            pre_parts_kernel,
            [shape((NX, 2 * TILE, TILE), BF16), shape((NZ * PIECE, TILE), BF16)],
            [smem()] + [vmem()] * 4 + [hbm()] * 2,
            4 * 512 * 3072 * 128,
            8000000,
            [
                pltpu.VMEM((LINE, TILE + ROOM, TILE), BF16),
                pltpu.VMEM((LINE, 4 * TILE, TILE), BF16),
                pltpu.SemaphoreType.DMA((12,)),
            ],
            limit=50,
        )(x, *tiles, blocks, turned)
    with jax.named_scope("sum_pre_x"):
        parts = lax.all_to_all(parts, "blk", 0, 0, tiled=True, axis_index_groups=X_GROUPS)
    with jax.named_scope("spread"):
        spread, weights = call(
            spread_kernel,
            [shape((NREP, TILE, TILE), BF16), shape((NZ * PIECE + TILE, TILE), BF16)],
            [vmem()] * 3,
            500000,
            800000,
        )(degree, parts, w_out)
    with jax.named_scope("gather_spread"):
        spread = lax.all_to_all(spread, "rep", 0, 0, tiled=True)
    with jax.named_scope("gather_weights"):
        weights = lax.all_gather(weights, "blk", axis=0, tiled=False, axis_index_groups=X_GROUPS)
    with jax.named_scope("final"):
        return tuple(
            call(
                final_kernel,
                [shape((128, 1024), F32), shape((512, 128), F32), shape((128, 512), F32)],
                [vmem()] * 2 + [hbm()],
                2 * 128 * 1024 * 512,
                2500000,
                [pltpu.VMEM((NREP, 4 * TILE, TILE), BF16), pltpu.SemaphoreType.DMA((NREP,))],
                limit=56,
            )(weights, spread, weights_in)
        )


def solution(mesh):
    return jax.shard_map(
        local,
        mesh=mesh,
        in_specs=(
            P("blk", None),
            P("blk", "rep"),
            P("blk", "rep"),
            P("blk", None),
            P(None, "rep"),
            P("rep", None),
            P("blk", None, None, None),
            P("blk", None),
            P("blk"),
            P("blk"),
        ),
        out_specs=(P("rep", None), P(None, "rep"), P("blk", None)),
        check_vma=False,
    )
```

```python
import jax
import jax.numpy as jnp
from jax import lax
from jax.experimental import pallas as pl
from jax.experimental.pallas import tpu as pltpu
from jax.sharding import PartitionSpec as P

TILE = 128
NX, NZ, NC = 4, 12, 2
NREP = 8
LINE = NZ * NC
WIDE = LINE * TILE
PIECE = 24
CHUNK = NX * PIECE
ROOM = 32
BF16 = jnp.bfloat16
F32 = jnp.float32
MIB = 1024 * 1024
ACROSS = (((0,), (0,)), ((), ()))
BY_ROWS = (((1,), (1,)), ((), ()))


def blk_index(x, z, c):
    return (x * NZ + z) * NC + c


Z_GROUPS = [[blk_index(x, z, c) for z in range(NZ)] for x in range(NX) for c in range(NC)]
X_GROUPS = [[blk_index(x, z, c) for x in range(NX)] for z in range(NZ) for c in range(NC)]
LINE_GROUPS = [[x * LINE + p for p in range(LINE)] for x in range(NX)]


def along_x(k):
    return [(x * LINE + p, (x + k) % NX * LINE + p) for x in range(NX) for p in range(LINE)]


def vmem():
    return pl.BlockSpec(memory_space=pltpu.VMEM)


def smem():
    return pl.BlockSpec(memory_space=pltpu.SMEM)


def hbm():
    return pl.BlockSpec(memory_space=pltpu.HBM)


def call(kernel, out_shape, in_specs, flops, moved, scratch=(), limit=14):
    return pl.pallas_call(
        kernel,
        out_shape=out_shape,
        in_specs=in_specs,
        out_specs=jax.tree.map(lambda _: vmem(), out_shape),
        scratch_shapes=scratch,
        compiler_params=pltpu.CompilerParams(vmem_limit_bytes=limit * MIB),
        cost_estimate=pl.CostEstimate(flops=flops, bytes_accessed=moved, transcendentals=0),
    )


def column_scale(degree_ref):
    inv_root = 1.0 / jnp.sqrt(degree_ref[...].astype(F32))
    return jnp.broadcast_to(inv_root, (TILE, TILE)).T


def start_kernel(
    x_ref,
    count_ref,
    source_hbm,
    degree_hbm,
    grad_out_hbm,
    weight_out_hbm,
    agg_hidden_hbm,
    agg_input_hbm,
    tiles_hbm,
    t0_ref,
    t1_ref,
    t2_ref,
    t3_ref,
    scaled_ref,
    weight_ref,
    turned_ref,
    source_ref,
    degree_ref,
    grad_out_ref,
    weight_out_ref,
    agg_hidden_ref,
    agg_input_ref,
    tiles_ref,
    sems,
):
    pairs = (
        (source_hbm, source_ref),
        (tiles_hbm, tiles_ref),
        (degree_hbm, degree_ref),
        (agg_input_hbm, agg_input_ref),
        (grad_out_hbm, grad_out_ref),
        (weight_out_hbm, weight_out_ref),
        (agg_hidden_hbm, agg_hidden_ref),
    )
    copies = [pltpu.make_async_copy(there, here, sems.at[i]) for i, (there, here) in enumerate(pairs)]
    for copy in copies:
        copy.start()
    out_refs = (t0_ref, t1_ref, t2_ref, t3_ref)
    for out_ref in out_refs:
        out_ref[...] = jnp.zeros_like(out_ref)
    weight_ref[8 * TILE :] = jnp.zeros((NZ * CHUNK - 8 * TILE, TILE), BF16)
    for copy in copies:
        copy.wait()

    root = jnp.sqrt(degree_ref[...].astype(F32))
    for j in range(4):
        rows = slice(j * TILE, (j + 1) * TILE)
        turned_ref[rows] = (agg_input_ref[:, rows].astype(F32).T * root).astype(BF16)

    def step(slot, carry):
        source = source_ref[0, slot]
        line = lax.div(source, LINE)
        columns = pl.ds(pl.multiple_of((source - line * LINE) * TILE, TILE), TILE)
        away = (line - x_ref[0] + NX) & (NX - 1)
        for k, out_ref in enumerate(out_refs):

            @pl.when(away == k)
            def _():
                out_ref[:, columns] = tiles_ref[0, slot]

        return carry

    lax.fori_loop(0, count_ref[0], step, 0)
    delta = lax.dot_general(grad_out_ref[...], weight_out_ref[...], BY_ROWS, preferred_element_type=F32)
    scaled_ref[...] = (column_scale(degree_ref) * delta).astype(BF16)
    w_out = lax.dot_general(agg_hidden_ref[...], grad_out_ref[...], ACROSS, preferred_element_type=F32)
    for j in range(8):
        weight_ref[j * TILE : (j + 1) * TILE] = w_out[:, j * TILE : (j + 1) * TILE].astype(BF16)


def multiply(tiles_refs, blocks):
    return [jnp.dot(tiles_ref[...], blocks, preferred_element_type=F32).astype(BF16) for tiles_ref in tiles_refs]


def out_parts_kernel(x_ref, t0_ref, t1_ref, t2_ref, t3_ref, blocks_ref, weight_ref, out_ref):
    parts = multiply((t0_ref, t1_ref, t2_ref, t3_ref), blocks_ref[...])
    total = weight_ref[0].astype(F32)
    for j in range(1, NZ):
        total = total + weight_ref[j].astype(F32)
    for k in range(NX):
        out_ref[(x_ref[0] - k + NX) & (NX - 1), :TILE] = parts[k]
        piece = total[k * PIECE : (k + 1) * PIECE]
        piece = jnp.concatenate([piece, jnp.zeros((ROOM - PIECE, TILE), F32)], axis=0)
        out_ref[k, TILE:] = piece.astype(BF16)


def sum_lines(got_ref):
    return (got_ref[0].astype(F32) + got_ref[1].astype(F32)) + (got_ref[2].astype(F32) + got_ref[3].astype(F32))


def hidden_kernel(degree_ref, got_ref, pre_hidden_ref, out_ref):
    scale = column_scale(degree_ref)
    total = sum_lines(got_ref)
    grad_pre = jnp.where(pre_hidden_ref[...].astype(F32) > 0, scale * total[:TILE], 0.0).astype(BF16)
    out_ref[:TILE] = (scale * grad_pre.astype(F32)).astype(BF16)
    out_ref[TILE:] = total[TILE:].astype(BF16)


def pre_parts_kernel(
    x_ref, t0_ref, t1_ref, t2_ref, t3_ref, blocks_ref, turned_hbm, out_ref, weight_ref, turned_ref, sems
):
    copies = []
    for i in range(6):
        part = pl.ds(4 * i, 4)
        copies.append(pltpu.make_async_copy(turned_hbm.at[part], turned_ref.at[part], sems.at[i]))
        copies[-1].start()
    blocks = blocks_ref[:, :TILE].reshape(WIDE, TILE)
    parts = multiply((t0_ref, t1_ref, t2_ref, t3_ref), blocks)
    for k in range(NX):
        out_ref[(x_ref[0] - k + NX) & (NX - 1), :TILE] = parts[k]
    pieces = []
    for z in range(NZ):
        both = blocks_ref[2 * z, TILE:].astype(F32) + blocks_ref[2 * z + 1, TILE:].astype(F32)
        pieces.append(both[:PIECE])
    weight_ref[...] = jnp.concatenate(pieces, axis=0).astype(BF16)
    w_in = jnp.zeros((4 * TILE, TILE), F32)
    for p in range(0, LINE, 4):
        copies[p // 4].wait()
        turned = jnp.concatenate([turned_ref[p + i] for i in range(4)], axis=1)
        w_in = w_in + jnp.dot(turned, blocks[p * TILE : (p + 4) * TILE], preferred_element_type=F32)
    for k in range(NX):
        out_ref[k, TILE:] = w_in[k * TILE : (k + 1) * TILE].astype(BF16)


def spread_kernel(degree_ref, got_ref, w_out_ref, spread_ref, weight_ref):
    total = sum_lines(got_ref)
    spread = (column_scale(degree_ref) * total[:TILE]).astype(BF16)
    for j in range(NREP):
        spread_ref[j] = spread
    weight_ref[: NZ * PIECE] = w_out_ref[...]
    weight_ref[NZ * PIECE :] = total[TILE:].astype(BF16)


def final_kernel(weights_ref, spread_ref, weight_in_ref, w_out_ref, w_in_ref, input_ref):
    for x in range(NX):
        weights = weights_ref[x].astype(F32)
        for z in range(NZ):
            row = z * CHUNK + x * PIECE
            at, left = z * PIECE, min(PIECE, 8 * TILE - row)
            while left > 0:
                j, r = row // TILE, row % TILE
                n = min(left, TILE - r)
                w_out_ref[r : r + n, j * TILE : (j + 1) * TILE] = weights[at : at + n]
                row, at, left = row + n, at + n, left - n
        w_in_ref[x * TILE : (x + 1) * TILE] = weights[NZ * PIECE :]
    total = jnp.zeros((TILE, 512), F32)
    for k in range(NREP):
        total = total + lax.dot_general(spread_ref[k], weight_in_ref[k], BY_ROWS, preferred_element_type=F32)
    input_ref[...] = total


def local(
    grad_out,
    agg_hidden,
    pre_hidden,
    agg_input,
    weight_in,
    weight_out,
    edge_tiles,
    tile_source,
    tile_count,
    degree,
):
    shape = jax.ShapeDtypeStruct
    block = shape((TILE, TILE), BF16)
    x = (lax.axis_index("blk") // LINE).astype(jnp.int32).reshape(1)
    degree = degree.reshape(1, TILE)

    copied = [tile_source, degree, grad_out, weight_out, agg_hidden, agg_input, edge_tiles]
    homes = [pltpu.SMEM] + [pltpu.VMEM] * 6
    with jax.named_scope("start"):
        *tiles, scaled, weights, turned = call(
            start_kernel,
            [shape((TILE, WIDE), BF16)] * NX
            + [block, shape((NZ * CHUNK, TILE), BF16), shape((4 * TILE, TILE), BF16)],
            [smem()] * 2 + [hbm()] * 7,
            4 * 128 * 128 * 1024,
            6000000,
            [home(a.shape, a.dtype) for home, a in zip(homes, copied)] + [pltpu.SemaphoreType.DMA((7,))],
            limit=56,
        )(x, tile_count, *copied)
    with jax.named_scope("gather_input"):
        turned = lax.all_gather(turned, "blk", axis=0, tiled=False, axis_index_groups=LINE_GROUPS)
    with jax.named_scope("gather_weight_in"):
        weights_in = lax.all_gather(weight_in, "rep", axis=0, tiled=False)
    with jax.named_scope("exchange_tiles"):
        tiles = [tiles[0]] + [lax.ppermute(tiles[k], "blk", along_x(k)) for k in range(1, NX)]
    with jax.named_scope("sum_weights_z"):
        weights = weights.reshape(NZ, CHUNK, TILE)
        weights = lax.all_to_all(weights, "blk", 0, 0, tiled=True, axis_index_groups=Z_GROUPS)
    with jax.named_scope("gather_out"):
        blocks = lax.all_gather(scaled, "blk", axis=0, tiled=True, axis_index_groups=LINE_GROUPS)
    with jax.named_scope("out_parts"):
        parts = call(
            out_parts_kernel,
            shape((NX, TILE + ROOM, TILE), BF16),
            [smem()] + [vmem()] * 6,
            2 * 512 * 3072 * 128,
            4000000,
            limit=50,
        )(x, *tiles, blocks, weights)
    with jax.named_scope("sum_out_x"):
        parts = lax.all_to_all(parts, "blk", 0, 0, tiled=True, axis_index_groups=X_GROUPS)
    with jax.named_scope("hidden"):
        scaled = call(hidden_kernel, shape((TILE + ROOM, TILE), BF16), [vmem()] * 3, 1000000, 600000)(
            degree, parts, pre_hidden
        )
    scaled, turned = lax.optimization_barrier((scaled, turned))
    with jax.named_scope("gather_pre"):
        blocks = lax.all_gather(scaled, "blk", axis=0, tiled=False, axis_index_groups=LINE_GROUPS)
    with jax.named_scope("pre_parts"):
        parts, w_out = call(
            pre_parts_kernel,
            [shape((NX, 2 * TILE, TILE), BF16), shape((NZ * PIECE, TILE), BF16)],
            [smem()] + [vmem()] * 5 + [hbm()],
            4 * 512 * 3072 * 128,
            8000000,
            [pltpu.VMEM((LINE, 4 * TILE, TILE), BF16), pltpu.SemaphoreType.DMA((6,))],
            limit=48,
        )(x, *tiles, blocks, turned)
    with jax.named_scope("sum_pre_x"):
        parts = lax.all_to_all(parts, "blk", 0, 0, tiled=True, axis_index_groups=X_GROUPS)
    with jax.named_scope("spread"):
        spread, weights = call(
            spread_kernel,
            [shape((NREP, TILE, TILE), BF16), shape((NZ * PIECE + TILE, TILE), BF16)],
            [vmem()] * 3,
            500000,
            800000,
        )(degree, parts, w_out)
    with jax.named_scope("gather_spread"):
        spread = lax.all_to_all(spread, "rep", 0, 0, tiled=True)
    with jax.named_scope("gather_weights"):
        weights = lax.all_gather(weights, "blk", axis=0, tiled=False, axis_index_groups=X_GROUPS)
    with jax.named_scope("final"):
        return tuple(
            call(
                final_kernel,
                [shape((128, 1024), F32), shape((512, 128), F32), shape((128, 512), F32)],
                [vmem()] * 3,
                2 * 128 * 1024 * 512,
                2500000,
                limit=14,
            )(weights, spread, weights_in)
        )


def solution(mesh):
    return jax.shard_map(
        local,
        mesh=mesh,
        in_specs=(
            P("blk", None),
            P("blk", "rep"),
            P("blk", "rep"),
            P("blk", None),
            P(None, "rep"),
            P("rep", None),
            P("blk", None, None, None),
            P("blk", None),
            P("blk"),
            P("blk"),
        ),
        out_specs=(P("rep", None), P(None, "rep"), P("blk", None)),
        check_vma=False,
    )
```

```python
import jax
import jax.numpy as jnp
from jax import lax
from jax.experimental import pallas as pl
from jax.experimental.pallas import tpu as pltpu
from jax.sharding import PartitionSpec as P

TILE = 128
NX, NZ, NC = 4, 12, 2
NREP = 8
LINE = NZ * NC
WIDE = LINE * TILE
PIECE = 24
CHUNK = NX * PIECE
ROOM = 32
BF16 = jnp.bfloat16
F32 = jnp.float32
MIB = 1024 * 1024
ACROSS = (((0,), (0,)), ((), ()))
BY_ROWS = (((1,), (1,)), ((), ()))


def blk_index(x, z, c):
    return (x * NZ + z) * NC + c


Z_GROUPS = [[blk_index(x, z, c) for z in range(NZ)] for x in range(NX) for c in range(NC)]
X_GROUPS = [[blk_index(x, z, c) for x in range(NX)] for z in range(NZ) for c in range(NC)]
SIDE_GROUPS = [[blk_index(x, z, c) for x in range(NX) for c in range(NC)] for z in range(NZ)]
LINE_GROUPS = [[x * LINE + p for p in range(LINE)] for x in range(NX)]


def along_x(k):
    return [(x * LINE + p, (x + k) % NX * LINE + p) for x in range(NX) for p in range(LINE)]


def vmem():
    return pl.BlockSpec(memory_space=pltpu.VMEM)


def smem():
    return pl.BlockSpec(memory_space=pltpu.SMEM)


def hbm():
    return pl.BlockSpec(memory_space=pltpu.HBM)


def call(kernel, out_shape, in_specs, flops, moved, scratch=(), limit=14):
    return pl.pallas_call(
        kernel,
        out_shape=out_shape,
        in_specs=in_specs,
        out_specs=jax.tree.map(lambda _: vmem(), out_shape),
        scratch_shapes=scratch,
        compiler_params=pltpu.CompilerParams(vmem_limit_bytes=limit * MIB),
        cost_estimate=pl.CostEstimate(flops=flops, bytes_accessed=moved, transcendentals=0),
    )


def column_scale(degree_ref):
    inv_root = 1.0 / jnp.sqrt(degree_ref[...].astype(F32))
    return jnp.broadcast_to(inv_root, (TILE, TILE)).T


def start_kernel(
    me_ref,
    count_ref,
    source_hbm,
    degree_hbm,
    grad_out_hbm,
    weight_out_hbm,
    agg_hidden_hbm,
    agg_input_hbm,
    tiles_hbm,
    t0_ref,
    t1_ref,
    t2_ref,
    t3_ref,
    scaled_ref,
    weight_ref,
    turned_ref,
    source_ref,
    degree_ref,
    grad_out_ref,
    weight_out_ref,
    agg_hidden_ref,
    agg_input_ref,
    tiles_ref,
    sems,
):
    pairs = (
        (source_hbm, source_ref),
        (tiles_hbm, tiles_ref),
        (degree_hbm, degree_ref),
        (agg_input_hbm, agg_input_ref),
        (grad_out_hbm, grad_out_ref),
        (weight_out_hbm, weight_out_ref),
        (agg_hidden_hbm, agg_hidden_ref),
    )
    copies = [pltpu.make_async_copy(there, here, sems.at[i]) for i, (there, here) in enumerate(pairs)]
    for copy in copies:
        copy.start()
    out_refs = (t0_ref, t1_ref, t2_ref, t3_ref)
    for out_ref in out_refs:
        out_ref[...] = jnp.zeros_like(out_ref)
    weight_ref[8 * TILE :] = jnp.zeros((NZ * CHUNK - 8 * TILE, TILE), BF16)
    for copy in copies:
        copy.wait()

    root = jnp.sqrt(degree_ref[...].astype(F32))
    for j in range(4):
        rows = slice(j * TILE, (j + 1) * TILE)
        turned_ref[rows] = (agg_input_ref[:, rows].astype(F32).T * root).astype(BF16)

    x = lax.div(me_ref[0], LINE)

    def step(slot, carry):
        source = source_ref[0, slot]
        line = lax.div(source, LINE)
        columns = pl.ds(pl.multiple_of((source - line * LINE) * TILE, TILE), TILE)
        away = (line - x + NX) & (NX - 1)
        for k, out_ref in enumerate(out_refs):

            @pl.when(away == k)
            def _():
                out_ref[:, columns] = tiles_ref[0, slot]

        return carry

    lax.fori_loop(0, count_ref[0], step, 0)
    delta = lax.dot_general(grad_out_ref[...], weight_out_ref[...], BY_ROWS, preferred_element_type=F32)
    scaled_ref[...] = (column_scale(degree_ref) * delta).astype(BF16)
    w_out = lax.dot_general(agg_hidden_ref[...], grad_out_ref[...], ACROSS, preferred_element_type=F32)
    for j in range(8):
        weight_ref[j * TILE : (j + 1) * TILE] = w_out[:, j * TILE : (j + 1) * TILE].astype(BF16)


def multiply(tiles_refs, blocks):
    return [jnp.dot(tiles_ref[...], blocks, preferred_element_type=F32).astype(BF16) for tiles_ref in tiles_refs]


def out_parts_kernel(me_ref, t0_ref, t1_ref, t2_ref, t3_ref, blocks_ref, weight_ref, out_ref):
    parts = multiply((t0_ref, t1_ref, t2_ref, t3_ref), blocks_ref[...])
    total = weight_ref[0].astype(F32)
    for j in range(1, NZ):
        total = total + weight_ref[j].astype(F32)
    for k in range(NX):
        out_ref[(lax.div(me_ref[0], LINE) - k + NX) & (NX - 1), :TILE] = parts[k]
        piece = total[k * PIECE : (k + 1) * PIECE]
        piece = jnp.concatenate([piece, jnp.zeros((ROOM - PIECE, TILE), F32)], axis=0)
        out_ref[k, TILE:] = piece.astype(BF16)


def sum_lines(got_ref):
    return (got_ref[0].astype(F32) + got_ref[1].astype(F32)) + (got_ref[2].astype(F32) + got_ref[3].astype(F32))


def hidden_kernel(degree_ref, got_ref, pre_hidden_ref, out_ref):
    scale = column_scale(degree_ref)
    total = sum_lines(got_ref)
    grad_pre = jnp.where(pre_hidden_ref[...].astype(F32) > 0, scale * total[:TILE], 0.0).astype(BF16)
    out_ref[:TILE] = (scale * grad_pre.astype(F32)).astype(BF16)
    out_ref[TILE:] = total[TILE:].astype(BF16)


def pre_parts_kernel(me_ref, t0_ref, t1_ref, t2_ref, t3_ref, blocks_ref, turned_ref, out_ref, weight_ref):
    blocks = blocks_ref[:, :TILE].reshape(WIDE, TILE)
    parts = multiply((t0_ref, t1_ref, t2_ref, t3_ref), blocks)
    for k in range(NX):
        out_ref[(lax.div(me_ref[0], LINE) - k + NX) & (NX - 1), :TILE] = parts[k]
    pieces = []
    for z in range(NZ):
        both = blocks_ref[2 * z, TILE:].astype(F32) + blocks_ref[2 * z + 1, TILE:].astype(F32)
        pieces.append(both[:PIECE])
    weight_ref[...] = jnp.concatenate(pieces, axis=0).astype(BF16)
    core = me_ref[0] & 1
    w_in = jnp.zeros((4 * TILE, TILE), F32)
    for z in range(0, NZ, 2):
        turned = jnp.concatenate([turned_ref[z], turned_ref[z + 1]], axis=1)
        mine = jnp.concatenate([blocks_ref[2 * (z + i) + core, :TILE] for i in range(2)], axis=0)
        w_in = w_in + jnp.dot(turned, mine, preferred_element_type=F32)
    for k in range(NX):
        out_ref[k, TILE:] = w_in[k * TILE : (k + 1) * TILE].astype(BF16)


def spread_kernel(degree_ref, got_ref, w_out_ref, spread_ref, weight_ref):
    total = sum_lines(got_ref)
    spread = (column_scale(degree_ref) * total[:TILE]).astype(BF16)
    for j in range(NREP):
        spread_ref[j] = spread
    weight_ref[: NZ * PIECE] = w_out_ref[...]
    weight_ref[NZ * PIECE :] = total[TILE:].astype(BF16)


def final_kernel(weights_ref, spread_ref, weight_in_ref, w_out_ref, w_in_ref, input_ref):
    for x in range(NX):
        weights = weights_ref[2 * x].astype(F32)
        for z in range(NZ):
            row = z * CHUNK + x * PIECE
            at, left = z * PIECE, min(PIECE, 8 * TILE - row)
            while left > 0:
                j, r = row // TILE, row % TILE
                n = min(left, TILE - r)
                w_out_ref[r : r + n, j * TILE : (j + 1) * TILE] = weights[at : at + n]
                row, at, left = row + n, at + n, left - n
        w_in_ref[x * TILE : (x + 1) * TILE] = weights[NZ * PIECE :] + weights_ref[2 * x + 1, NZ * PIECE :].astype(F32)
    total = jnp.zeros((TILE, 512), F32)
    for k in range(NREP):
        total = total + lax.dot_general(spread_ref[k], weight_in_ref[k], BY_ROWS, preferred_element_type=F32)
    input_ref[...] = total


def local(
    grad_out,
    agg_hidden,
    pre_hidden,
    agg_input,
    weight_in,
    weight_out,
    edge_tiles,
    tile_source,
    tile_count,
    degree,
):
    shape = jax.ShapeDtypeStruct
    block = shape((TILE, TILE), BF16)
    me = lax.axis_index("blk").astype(jnp.int32).reshape(1)
    degree = degree.reshape(1, TILE)

    copied = [tile_source, degree, grad_out, weight_out, agg_hidden, agg_input, edge_tiles]
    homes = [pltpu.SMEM] + [pltpu.VMEM] * 6
    with jax.named_scope("start"):
        *tiles, scaled, weights, turned = call(
            start_kernel,
            [shape((TILE, WIDE), BF16)] * NX
            + [block, shape((NZ * CHUNK, TILE), BF16), shape((4 * TILE, TILE), BF16)],
            [smem()] * 2 + [hbm()] * 7,
            4 * 128 * 128 * 1024,
            6000000,
            [home(a.shape, a.dtype) for home, a in zip(homes, copied)] + [pltpu.SemaphoreType.DMA((7,))],
            limit=56,
        )(me, tile_count, *copied)
    with jax.named_scope("gather_input"):
        turned = lax.all_gather(turned, "blk", axis=0, tiled=False, axis_index_groups=Z_GROUPS)
    with jax.named_scope("gather_weight_in"):
        weights_in = lax.all_gather(weight_in, "rep", axis=0, tiled=False)
    with jax.named_scope("exchange_tiles"):
        tiles = [tiles[0]] + [lax.ppermute(tiles[k], "blk", along_x(k)) for k in range(1, NX)]
    with jax.named_scope("sum_weights_z"):
        weights = weights.reshape(NZ, CHUNK, TILE)
        weights = lax.all_to_all(weights, "blk", 0, 0, tiled=True, axis_index_groups=Z_GROUPS)
    with jax.named_scope("gather_out"):
        blocks = lax.all_gather(scaled, "blk", axis=0, tiled=True, axis_index_groups=LINE_GROUPS)
    with jax.named_scope("out_parts"):
        parts = call(
            out_parts_kernel,
            shape((NX, TILE + ROOM, TILE), BF16),
            [smem()] + [vmem()] * 6,
            2 * 512 * 3072 * 128,
            4000000,
            limit=50,
        )(me, *tiles, blocks, weights)
    with jax.named_scope("sum_out_x"):
        parts = lax.all_to_all(parts, "blk", 0, 0, tiled=True, axis_index_groups=X_GROUPS)
    with jax.named_scope("hidden"):
        scaled = call(hidden_kernel, shape((TILE + ROOM, TILE), BF16), [vmem()] * 3, 1000000, 600000)(
            degree, parts, pre_hidden
        )
    scaled, turned = lax.optimization_barrier((scaled, turned))
    with jax.named_scope("gather_pre"):
        blocks = lax.all_gather(scaled, "blk", axis=0, tiled=False, axis_index_groups=LINE_GROUPS)
    with jax.named_scope("pre_parts"):
        parts, w_out = call(
            pre_parts_kernel,
            [shape((NX, 2 * TILE, TILE), BF16), shape((NZ * PIECE, TILE), BF16)],
            [smem()] + [vmem()] * 6,
            4 * 512 * 3072 * 128,
            8000000,
            limit=44,
        )(me, *tiles, blocks, turned)
    with jax.named_scope("sum_pre_x"):
        parts = lax.all_to_all(parts, "blk", 0, 0, tiled=True, axis_index_groups=X_GROUPS)
    with jax.named_scope("spread"):
        spread, weights = call(
            spread_kernel,
            [shape((NREP, TILE, TILE), BF16), shape((NZ * PIECE + TILE, TILE), BF16)],
            [vmem()] * 3,
            500000,
            800000,
        )(degree, parts, w_out)
    with jax.named_scope("gather_spread"):
        spread = lax.all_to_all(spread, "rep", 0, 0, tiled=True)
    with jax.named_scope("gather_weights"):
        weights = lax.all_gather(weights, "blk", axis=0, tiled=False, axis_index_groups=SIDE_GROUPS)
    with jax.named_scope("final"):
        return tuple(
            call(
                final_kernel,
                [shape((128, 1024), F32), shape((512, 128), F32), shape((128, 512), F32)],
                [vmem()] * 3,
                2 * 128 * 1024 * 512,
                2500000,
                limit=14,
            )(weights, spread, weights_in)
        )


def solution(mesh):
    return jax.shard_map(
        local,
        mesh=mesh,
        in_specs=(
            P("blk", None),
            P("blk", "rep"),
            P("blk", "rep"),
            P("blk", None),
            P(None, "rep"),
            P("rep", None),
            P("blk", None, None, None),
            P("blk", None),
            P("blk"),
            P("blk"),
        ),
        out_specs=(P("rep", None), P(None, "rep"), P("blk", None)),
        check_vma=False,
    )
```

```python
import jax
import jax.numpy as jnp
from jax import lax
from jax.experimental import pallas as pl
from jax.experimental.pallas import tpu as pltpu
from jax.sharding import PartitionSpec as P

TILE = 128
NX, NZ, NC = 4, 12, 2
NREP = 8
LINE = NZ * NC
WIDE = LINE * TILE
PIECE = 24
CHUNK = NX * PIECE
ROOM = 32
BF16 = jnp.bfloat16
F32 = jnp.float32
MIB = 1024 * 1024
ACROSS = (((0,), (0,)), ((), ()))
BY_ROWS = (((1,), (1,)), ((), ()))


def blk_index(x, z, c):
    return (x * NZ + z) * NC + c


Z_GROUPS = [[blk_index(x, z, c) for z in range(NZ)] for x in range(NX) for c in range(NC)]
X_GROUPS = [[blk_index(x, z, c) for x in range(NX)] for z in range(NZ) for c in range(NC)]
SIDE_GROUPS = [[blk_index(x, z, c) for x in range(NX) for c in range(NC)] for z in range(NZ)]
LINE_GROUPS = [[x * LINE + p for p in range(LINE)] for x in range(NX)]


def along_x(k):
    return [(x * LINE + p, (x + k) % NX * LINE + p) for x in range(NX) for p in range(LINE)]


def vmem():
    return pl.BlockSpec(memory_space=pltpu.VMEM)


def smem():
    return pl.BlockSpec(memory_space=pltpu.SMEM)


def hbm():
    return pl.BlockSpec(memory_space=pltpu.HBM)


def call(kernel, out_shape, in_specs, flops, moved, scratch=(), limit=14):
    return pl.pallas_call(
        kernel,
        out_shape=out_shape,
        in_specs=in_specs,
        out_specs=jax.tree.map(lambda _: vmem(), out_shape),
        scratch_shapes=scratch,
        compiler_params=pltpu.CompilerParams(vmem_limit_bytes=limit * MIB),
        cost_estimate=pl.CostEstimate(flops=flops, bytes_accessed=moved, transcendentals=0),
    )


def column_scale(degree_ref):
    inv_root = 1.0 / jnp.sqrt(degree_ref[...].astype(F32))
    return jnp.broadcast_to(inv_root, (TILE, TILE)).T


def start_kernel(
    me_ref,
    count_ref,
    source_hbm,
    degree_hbm,
    grad_out_hbm,
    weight_out_hbm,
    agg_hidden_hbm,
    agg_input_hbm,
    tiles_hbm,
    t0_ref,
    t1_ref,
    t2_ref,
    t3_ref,
    scaled_ref,
    weight_ref,
    turned_ref,
    source_ref,
    degree_ref,
    grad_out_ref,
    weight_out_ref,
    agg_hidden_ref,
    agg_input_ref,
    tiles_ref,
    sems,
):
    pairs = (
        (source_hbm, source_ref),
        (tiles_hbm, tiles_ref),
        (degree_hbm, degree_ref),
        (agg_input_hbm, agg_input_ref),
        (grad_out_hbm, grad_out_ref),
        (weight_out_hbm, weight_out_ref),
        (agg_hidden_hbm, agg_hidden_ref),
    )
    copies = [pltpu.make_async_copy(there, here, sems.at[i]) for i, (there, here) in enumerate(pairs)]
    for copy in copies:
        copy.start()
    out_refs = (t0_ref, t1_ref, t2_ref, t3_ref)
    for out_ref in out_refs:
        out_ref[...] = jnp.zeros_like(out_ref)
    weight_ref[8 * TILE :] = jnp.zeros((NZ * CHUNK - 8 * TILE, TILE), BF16)
    for copy in copies:
        copy.wait()

    root = jnp.sqrt(degree_ref[...].astype(F32))
    for j in range(4):
        rows = slice(j * TILE, (j + 1) * TILE)
        turned_ref[rows] = (agg_input_ref[:, rows].astype(F32).T * root).astype(BF16)

    x = lax.div(me_ref[0], LINE)

    def step(slot, carry):
        source = source_ref[0, slot]
        line = lax.div(source, LINE)
        columns = pl.ds(pl.multiple_of((source - line * LINE) * TILE, TILE), TILE)
        away = (line - x + NX) & (NX - 1)
        for k, out_ref in enumerate(out_refs):

            @pl.when(away == k)
            def _():
                out_ref[:, columns] = tiles_ref[0, slot]

        return carry

    lax.fori_loop(0, count_ref[0], step, 0)
    delta = lax.dot_general(grad_out_ref[...], weight_out_ref[...], BY_ROWS, preferred_element_type=F32)
    scaled_ref[...] = (column_scale(degree_ref) * delta).astype(BF16)
    w_out = lax.dot_general(agg_hidden_ref[...], grad_out_ref[...], ACROSS, preferred_element_type=F32)
    for j in range(8):
        weight_ref[j * TILE : (j + 1) * TILE] = w_out[:, j * TILE : (j + 1) * TILE].astype(BF16)


def multiply(tiles_refs, blocks):
    return [jnp.dot(tiles_ref[...], blocks, preferred_element_type=F32).astype(BF16) for tiles_ref in tiles_refs]


def out_parts_kernel(me_ref, t0_ref, t2_ref, t3_ref, t1_ref, blocks_ref, weight_ref, out_ref):
    parts = multiply((t0_ref, t1_ref, t2_ref, t3_ref), blocks_ref[...])
    total = weight_ref[0].astype(F32)
    for j in range(1, NZ):
        total = total + weight_ref[j].astype(F32)
    for k in range(NX):
        out_ref[(lax.div(me_ref[0], LINE) - k + NX) & (NX - 1), :TILE] = parts[k]
        piece = total[k * PIECE : (k + 1) * PIECE]
        piece = jnp.concatenate([piece, jnp.zeros((ROOM - PIECE, TILE), F32)], axis=0)
        out_ref[k, TILE:] = piece.astype(BF16)


def sum_lines(got_ref):
    return (got_ref[0].astype(F32) + got_ref[1].astype(F32)) + (got_ref[2].astype(F32) + got_ref[3].astype(F32))


def hidden_kernel(degree_ref, got_ref, pre_hidden_ref, out_ref):
    scale = column_scale(degree_ref)
    total = sum_lines(got_ref)
    grad_pre = jnp.where(pre_hidden_ref[...].astype(F32) > 0, scale * total[:TILE], 0.0).astype(BF16)
    out_ref[:TILE] = (scale * grad_pre.astype(F32)).astype(BF16)
    out_ref[TILE:] = total[TILE:].astype(BF16)


def pre_parts_kernel(me_ref, t0_ref, t2_ref, t3_ref, t1_ref, blocks_ref, turned_ref, out_ref, weight_ref):
    blocks = blocks_ref[:, :TILE].reshape(WIDE, TILE)
    parts = multiply((t0_ref, t1_ref, t2_ref, t3_ref), blocks)
    for k in range(NX):
        out_ref[(lax.div(me_ref[0], LINE) - k + NX) & (NX - 1), :TILE] = parts[k]
    pieces = []
    for z in range(NZ):
        both = blocks_ref[2 * z, TILE:].astype(F32) + blocks_ref[2 * z + 1, TILE:].astype(F32)
        pieces.append(both[:PIECE])
    weight_ref[...] = jnp.concatenate(pieces, axis=0).astype(BF16)
    core = me_ref[0] & 1
    w_in = jnp.zeros((4 * TILE, TILE), F32)
    for z in range(0, NZ, 2):
        turned = jnp.concatenate([turned_ref[z], turned_ref[z + 1]], axis=1)
        mine = jnp.concatenate([blocks_ref[2 * (z + i) + core, :TILE] for i in range(2)], axis=0)
        w_in = w_in + jnp.dot(turned, mine, preferred_element_type=F32)
    for k in range(NX):
        out_ref[k, TILE:] = w_in[k * TILE : (k + 1) * TILE].astype(BF16)


def spread_kernel(degree_ref, got_ref, w_out_ref, spread_ref, weight_ref):
    total = sum_lines(got_ref)
    spread = (column_scale(degree_ref) * total[:TILE]).astype(BF16)
    for j in range(NREP):
        spread_ref[j] = spread
    weight_ref[: NZ * PIECE] = w_out_ref[...]
    weight_ref[NZ * PIECE :] = total[TILE:].astype(BF16)


def final_kernel(weights_ref, spread_ref, weight_in_ref, w_out_ref, w_in_ref, input_ref):
    for x in range(NX):
        weights = weights_ref[2 * x].astype(F32)
        for z in range(NZ):
            row = z * CHUNK + x * PIECE
            at, left = z * PIECE, min(PIECE, 8 * TILE - row)
            while left > 0:
                j, r = row // TILE, row % TILE
                n = min(left, TILE - r)
                w_out_ref[r : r + n, j * TILE : (j + 1) * TILE] = weights[at : at + n]
                row, at, left = row + n, at + n, left - n
        w_in_ref[x * TILE : (x + 1) * TILE] = weights[NZ * PIECE :] + weights_ref[2 * x + 1, NZ * PIECE :].astype(F32)
    total = jnp.zeros((TILE, 512), F32)
    for k in range(NREP):
        total = total + lax.dot_general(spread_ref[k], weight_in_ref[k], BY_ROWS, preferred_element_type=F32)
    input_ref[...] = total


def local(
    grad_out,
    agg_hidden,
    pre_hidden,
    agg_input,
    weight_in,
    weight_out,
    edge_tiles,
    tile_source,
    tile_count,
    degree,
):
    shape = jax.ShapeDtypeStruct
    block = shape((TILE, TILE), BF16)
    me = lax.axis_index("blk").astype(jnp.int32).reshape(1)
    degree = degree.reshape(1, TILE)

    copied = [tile_source, degree, grad_out, weight_out, agg_hidden, agg_input, edge_tiles]
    homes = [pltpu.SMEM] + [pltpu.VMEM] * 6
    with jax.named_scope("start"):
        *tiles, scaled, weights, turned = call(
            start_kernel,
            [shape((TILE, WIDE), BF16)] * NX
            + [block, shape((NZ * CHUNK, TILE), BF16), shape((4 * TILE, TILE), BF16)],
            [smem()] * 2 + [hbm()] * 7,
            4 * 128 * 128 * 1024,
            6000000,
            [home(a.shape, a.dtype) for home, a in zip(homes, copied)] + [pltpu.SemaphoreType.DMA((7,))],
            limit=56,
        )(me, tile_count, *copied)
    with jax.named_scope("gather_input"):
        turned = lax.all_gather(turned, "blk", axis=0, tiled=False, axis_index_groups=Z_GROUPS)
    with jax.named_scope("gather_weight_in"):
        weights_in = lax.all_gather(weight_in, "rep", axis=0, tiled=False)
    with jax.named_scope("exchange_tiles"):
        far, left, right = (lax.ppermute(tiles[k], "blk", along_x(k)) for k in (2, 3, 1))
        tiles = [tiles[0], far, left, right]
    with jax.named_scope("sum_weights_z"):
        weights = weights.reshape(NZ, CHUNK, TILE)
        weights = lax.all_to_all(weights, "blk", 0, 0, tiled=True, axis_index_groups=Z_GROUPS)
    with jax.named_scope("gather_out"):
        blocks = lax.all_gather(scaled, "blk", axis=0, tiled=True, axis_index_groups=LINE_GROUPS)
    with jax.named_scope("out_parts"):
        parts = call(
            out_parts_kernel,
            shape((NX, TILE + ROOM, TILE), BF16),
            [smem()] + [vmem()] * 6,
            2 * 512 * 3072 * 128,
            4000000,
            limit=50,
        )(me, *tiles, blocks, weights)
    with jax.named_scope("sum_out_x"):
        parts = lax.all_to_all(parts, "blk", 0, 0, tiled=True, axis_index_groups=X_GROUPS)
    with jax.named_scope("hidden"):
        scaled = call(hidden_kernel, shape((TILE + ROOM, TILE), BF16), [vmem()] * 3, 1000000, 600000)(
            degree, parts, pre_hidden
        )
    scaled, turned = lax.optimization_barrier((scaled, turned))
    with jax.named_scope("gather_pre"):
        blocks = lax.all_gather(scaled, "blk", axis=0, tiled=False, axis_index_groups=LINE_GROUPS)
    with jax.named_scope("pre_parts"):
        parts, w_out = call(
            pre_parts_kernel,
            [shape((NX, 2 * TILE, TILE), BF16), shape((NZ * PIECE, TILE), BF16)],
            [smem()] + [vmem()] * 6,
            4 * 512 * 3072 * 128,
            8000000,
            limit=44,
        )(me, *tiles, blocks, turned)
    with jax.named_scope("sum_pre_x"):
        parts = lax.all_to_all(parts, "blk", 0, 0, tiled=True, axis_index_groups=X_GROUPS)
    with jax.named_scope("spread"):
        spread, weights = call(
            spread_kernel,
            [shape((NREP, TILE, TILE), BF16), shape((NZ * PIECE + TILE, TILE), BF16)],
            [vmem()] * 3,
            500000,
            800000,
        )(degree, parts, w_out)
    with jax.named_scope("gather_spread"):
        spread = lax.all_to_all(spread, "rep", 0, 0, tiled=True)
    with jax.named_scope("gather_weights"):
        weights = lax.all_gather(weights, "blk", axis=0, tiled=False, axis_index_groups=SIDE_GROUPS)
    with jax.named_scope("final"):
        return tuple(
            call(
                final_kernel,
                [shape((128, 1024), F32), shape((512, 128), F32), shape((128, 512), F32)],
                [vmem()] * 3,
                2 * 128 * 1024 * 512,
                2500000,
                limit=14,
            )(weights, spread, weights_in)
        )


def solution(mesh):
    return jax.shard_map(
        local,
        mesh=mesh,
        in_specs=(
            P("blk", None),
            P("blk", "rep"),
            P("blk", "rep"),
            P("blk", None),
            P(None, "rep"),
            P("rep", None),
            P("blk", None, None, None),
            P("blk", None),
            P("blk"),
            P("blk"),
        ),
        out_specs=(P("rep", None), P(None, "rep"), P("blk", None)),
        check_vma=False,
    )
```

```python
import jax
import jax.numpy as jnp
from jax import lax
from jax.experimental import pallas as pl
from jax.experimental.pallas import tpu as pltpu
from jax.sharding import PartitionSpec as P

TILE = 128
NX, NZ, NC = 4, 12, 2
NREP = 8
LINE = NZ * NC
WIDE = LINE * TILE
PIECE = 24
CHUNK = NX * PIECE
ROOM = 32
BF16 = jnp.bfloat16
F32 = jnp.float32
MIB = 1024 * 1024
ACROSS = (((0,), (0,)), ((), ()))
BY_ROWS = (((1,), (1,)), ((), ()))


def blk_index(x, z, c):
    return (x * NZ + z) * NC + c


Z_GROUPS = [[blk_index(x, z, c) for z in range(NZ)] for x in range(NX) for c in range(NC)]
X_GROUPS = [[blk_index(x, z, c) for x in range(NX)] for z in range(NZ) for c in range(NC)]
SIDE_GROUPS = [[blk_index(x, z, c) for x in range(NX) for c in range(NC)] for z in range(NZ)]
LINE_GROUPS = [[x * LINE + p for p in range(LINE)] for x in range(NX)]


def along_x(k):
    return [(x * LINE + p, (x + k) % NX * LINE + p) for x in range(NX) for p in range(LINE)]


def vmem():
    return pl.BlockSpec(memory_space=pltpu.VMEM)


def smem():
    return pl.BlockSpec(memory_space=pltpu.SMEM)


def hbm():
    return pl.BlockSpec(memory_space=pltpu.HBM)


def call(kernel, out_shape, in_specs, flops, moved, scratch=(), limit=14):
    return pl.pallas_call(
        kernel,
        out_shape=out_shape,
        in_specs=in_specs,
        out_specs=jax.tree.map(lambda _: vmem(), out_shape),
        scratch_shapes=scratch,
        compiler_params=pltpu.CompilerParams(vmem_limit_bytes=limit * MIB),
        cost_estimate=pl.CostEstimate(flops=flops, bytes_accessed=moved, transcendentals=0),
    )


def column_scale(degree_ref):
    inv_root = 1.0 / jnp.sqrt(degree_ref[...].astype(F32))
    return jnp.broadcast_to(inv_root, (TILE, TILE)).T


def start_kernel(
    me_ref,
    count_ref,
    source_hbm,
    degree_hbm,
    grad_out_hbm,
    weight_out_hbm,
    agg_hidden_hbm,
    agg_input_hbm,
    tiles_hbm,
    t0_ref,
    t1_ref,
    t2_ref,
    t3_ref,
    scaled_ref,
    weight_ref,
    turned_ref,
    source_ref,
    degree_ref,
    grad_out_ref,
    weight_out_ref,
    agg_hidden_ref,
    agg_input_ref,
    tiles_ref,
    sems,
):
    pairs = (
        (source_hbm, source_ref),
        (tiles_hbm, tiles_ref),
        (degree_hbm, degree_ref),
        (agg_input_hbm, agg_input_ref),
        (grad_out_hbm, grad_out_ref),
        (weight_out_hbm, weight_out_ref),
        (agg_hidden_hbm, agg_hidden_ref),
    )
    copies = [pltpu.make_async_copy(there, here, sems.at[i]) for i, (there, here) in enumerate(pairs)]
    for copy in copies:
        copy.start()
    out_refs = (t0_ref, t1_ref, t2_ref, t3_ref)
    for out_ref in out_refs:
        out_ref[...] = jnp.zeros_like(out_ref)
    weight_ref[8 * TILE :] = jnp.zeros((NZ * CHUNK - 8 * TILE, TILE), BF16)
    for copy in copies:
        copy.wait()

    root = jnp.sqrt(degree_ref[...].astype(F32))
    for j in range(4):
        rows = slice(j * TILE, (j + 1) * TILE)
        turned_ref[rows] = (agg_input_ref[:, rows].astype(F32).T * root).astype(BF16)

    x = lax.div(me_ref[0], LINE)

    def step(slot, carry):
        source = source_ref[0, slot]
        line = lax.div(source, LINE)
        columns = pl.ds(pl.multiple_of((source - line * LINE) * TILE, TILE), TILE)
        away = (line - x + NX) & (NX - 1)
        for k, out_ref in enumerate(out_refs):

            @pl.when(away == k)
            def _():
                out_ref[:, columns] = tiles_ref[0, slot]

        return carry

    lax.fori_loop(0, count_ref[0], step, 0)
    delta = lax.dot_general(grad_out_ref[...], weight_out_ref[...], BY_ROWS, preferred_element_type=F32)
    scaled_ref[...] = (column_scale(degree_ref) * delta).astype(BF16)
    w_out = lax.dot_general(agg_hidden_ref[...], grad_out_ref[...], ACROSS, preferred_element_type=F32)
    for j in range(8):
        weight_ref[j * TILE : (j + 1) * TILE] = w_out[:, j * TILE : (j + 1) * TILE].astype(BF16)


def multiply(tiles_refs, blocks):
    return [jnp.dot(tiles_ref[...], blocks, preferred_element_type=F32).astype(BF16) for tiles_ref in tiles_refs]


def out_parts_kernel(me_ref, t0_ref, t2_ref, t3_ref, t1_ref, blocks_ref, weight_ref, out_ref):
    parts = multiply((t0_ref, t1_ref, t2_ref, t3_ref), blocks_ref[...])
    total = weight_ref[0].astype(F32)
    for j in range(1, NZ):
        total = total + weight_ref[j].astype(F32)
    for k in range(NX):
        out_ref[(lax.div(me_ref[0], LINE) - k + NX) & (NX - 1), :TILE] = parts[k]
        piece = total[k * PIECE : (k + 1) * PIECE]
        piece = jnp.concatenate([piece, jnp.zeros((ROOM - PIECE, TILE), F32)], axis=0)
        out_ref[k, TILE:] = piece.astype(BF16)


def sum_lines(got_ref):
    return (got_ref[0].astype(F32) + got_ref[1].astype(F32)) + (got_ref[2].astype(F32) + got_ref[3].astype(F32))


def hidden_kernel(degree_ref, got_ref, pre_hidden_ref, out_ref):
    scale = column_scale(degree_ref)
    total = sum_lines(got_ref)
    grad_pre = jnp.where(pre_hidden_ref[...].astype(F32) > 0, scale * total[:TILE], 0.0).astype(BF16)
    out_ref[:TILE] = (scale * grad_pre.astype(F32)).astype(BF16)
    out_ref[TILE:] = total[TILE:].astype(BF16)


def pre_parts_kernel(
    me_ref, t0_ref, t2_ref, t3_ref, t1_ref, blocks_ref, turned_hbm, out_ref, weight_ref, turned_ref, sems
):
    copies = []
    for i in range(NZ // 2):
        part = pl.ds(2 * i, 2)
        copies.append(pltpu.make_async_copy(turned_hbm.at[part], turned_ref.at[part], sems.at[i]))
        copies[-1].start()
    blocks = blocks_ref[:, :TILE].reshape(WIDE, TILE)
    parts = multiply((t0_ref, t1_ref, t2_ref, t3_ref), blocks)
    for k in range(NX):
        out_ref[(lax.div(me_ref[0], LINE) - k + NX) & (NX - 1), :TILE] = parts[k]
    pieces = []
    for z in range(NZ):
        both = blocks_ref[2 * z, TILE:].astype(F32) + blocks_ref[2 * z + 1, TILE:].astype(F32)
        pieces.append(both[:PIECE])
    weight_ref[...] = jnp.concatenate(pieces, axis=0).astype(BF16)
    core = me_ref[0] & 1
    w_in = jnp.zeros((4 * TILE, TILE), F32)
    for z in range(0, NZ, 2):
        copies[z // 2].wait()
        turned = jnp.concatenate([turned_ref[z], turned_ref[z + 1]], axis=1)
        mine = jnp.concatenate([blocks_ref[2 * (z + i) + core, :TILE] for i in range(2)], axis=0)
        w_in = w_in + jnp.dot(turned, mine, preferred_element_type=F32)
    for k in range(NX):
        out_ref[k, TILE:] = w_in[k * TILE : (k + 1) * TILE].astype(BF16)


def spread_kernel(degree_ref, got_ref, w_out_ref, spread_ref, weight_ref):
    total = sum_lines(got_ref)
    spread = (column_scale(degree_ref) * total[:TILE]).astype(BF16)
    for j in range(NREP):
        spread_ref[j] = spread
    weight_ref[: NZ * PIECE] = w_out_ref[...]
    weight_ref[NZ * PIECE :] = total[TILE:].astype(BF16)


def final_kernel(weights_ref, spread_ref, weight_in_ref, w_out_ref, w_in_ref, input_ref):
    for x in range(NX):
        weights = weights_ref[2 * x].astype(F32)
        for z in range(NZ):
            row = z * CHUNK + x * PIECE
            at, left = z * PIECE, min(PIECE, 8 * TILE - row)
            while left > 0:
                j, r = row // TILE, row % TILE
                n = min(left, TILE - r)
                w_out_ref[r : r + n, j * TILE : (j + 1) * TILE] = weights[at : at + n]
                row, at, left = row + n, at + n, left - n
        w_in_ref[x * TILE : (x + 1) * TILE] = weights[NZ * PIECE :] + weights_ref[2 * x + 1, NZ * PIECE :].astype(F32)
    total = jnp.zeros((TILE, 512), F32)
    for k in range(NREP):
        total = total + lax.dot_general(spread_ref[k], weight_in_ref[k], BY_ROWS, preferred_element_type=F32)
    input_ref[...] = total


def local(
    grad_out,
    agg_hidden,
    pre_hidden,
    agg_input,
    weight_in,
    weight_out,
    edge_tiles,
    tile_source,
    tile_count,
    degree,
):
    shape = jax.ShapeDtypeStruct
    block = shape((TILE, TILE), BF16)
    me = lax.axis_index("blk").astype(jnp.int32).reshape(1)
    degree = degree.reshape(1, TILE)

    copied = [tile_source, degree, grad_out, weight_out, agg_hidden, agg_input, edge_tiles]
    homes = [pltpu.SMEM] + [pltpu.VMEM] * 6
    with jax.named_scope("start"):
        *tiles, scaled, weights, turned = call(
            start_kernel,
            [shape((TILE, WIDE), BF16)] * NX
            + [block, shape((NZ * CHUNK, TILE), BF16), shape((4 * TILE, TILE), BF16)],
            [smem()] * 2 + [hbm()] * 7,
            4 * 128 * 128 * 1024,
            6000000,
            [home(a.shape, a.dtype) for home, a in zip(homes, copied)] + [pltpu.SemaphoreType.DMA((7,))],
            limit=56,
        )(me, tile_count, *copied)
    with jax.named_scope("gather_input"):
        turned = lax.all_gather(turned, "blk", axis=0, tiled=False, axis_index_groups=Z_GROUPS)
    with jax.named_scope("gather_weight_in"):
        weights_in = lax.all_gather(weight_in, "rep", axis=0, tiled=False)
    with jax.named_scope("exchange_tiles"):
        far, left, right = (lax.ppermute(tiles[k], "blk", along_x(k)) for k in (2, 3, 1))
        tiles = [tiles[0], far, left, right]
    with jax.named_scope("sum_weights_z"):
        weights = weights.reshape(NZ, CHUNK, TILE)
        weights = lax.all_to_all(weights, "blk", 0, 0, tiled=True, axis_index_groups=Z_GROUPS)
    with jax.named_scope("gather_out"):
        blocks = lax.all_gather(scaled, "blk", axis=0, tiled=True, axis_index_groups=LINE_GROUPS)
    with jax.named_scope("out_parts"):
        parts = call(
            out_parts_kernel,
            shape((NX, TILE + ROOM, TILE), BF16),
            [smem()] + [vmem()] * 6,
            2 * 512 * 3072 * 128,
            4000000,
            limit=50,
        )(me, *tiles, blocks, weights)
    with jax.named_scope("sum_out_x"):
        parts = lax.all_to_all(parts, "blk", 0, 0, tiled=True, axis_index_groups=X_GROUPS)
    with jax.named_scope("hidden"):
        scaled = call(hidden_kernel, shape((TILE + ROOM, TILE), BF16), [vmem()] * 3, 1000000, 600000)(
            degree, parts, pre_hidden
        )
    with jax.named_scope("gather_pre"):
        blocks = lax.all_gather(scaled, "blk", axis=0, tiled=False, axis_index_groups=LINE_GROUPS)
    with jax.named_scope("pre_parts"):
        parts, w_out = call(
            pre_parts_kernel,
            [shape((NX, 2 * TILE, TILE), BF16), shape((NZ * PIECE, TILE), BF16)],
            [smem()] + [vmem()] * 5 + [hbm()],
            4 * 512 * 3072 * 128,
            8000000,
            scratch=[pltpu.VMEM((NZ, 4 * TILE, TILE), BF16), pltpu.SemaphoreType.DMA((NZ // 2,))],
            limit=50,
        )(me, *tiles, blocks, turned)
    with jax.named_scope("sum_pre_x"):
        parts = lax.all_to_all(parts, "blk", 0, 0, tiled=True, axis_index_groups=X_GROUPS)
    with jax.named_scope("spread"):
        spread, weights = call(
            spread_kernel,
            [shape((NREP, TILE, TILE), BF16), shape((NZ * PIECE + TILE, TILE), BF16)],
            [vmem()] * 3,
            500000,
            800000,
        )(degree, parts, w_out)
    with jax.named_scope("gather_spread"):
        spread = lax.all_to_all(spread, "rep", 0, 0, tiled=True)
    with jax.named_scope("gather_weights"):
        weights = lax.all_gather(weights, "blk", axis=0, tiled=False, axis_index_groups=SIDE_GROUPS)
    with jax.named_scope("final"):
        return tuple(
            call(
                final_kernel,
                [shape((128, 1024), F32), shape((512, 128), F32), shape((128, 512), F32)],
                [vmem()] * 3,
                2 * 128 * 1024 * 512,
                2500000,
                limit=14,
            )(weights, spread, weights_in)
        )


def solution(mesh):
    return jax.shard_map(
        local,
        mesh=mesh,
        in_specs=(
            P("blk", None),
            P("blk", "rep"),
            P("blk", "rep"),
            P("blk", None),
            P(None, "rep"),
            P("rep", None),
            P("blk", None, None, None),
            P("blk", None),
            P("blk"),
            P("blk"),
        ),
        out_specs=(P("rep", None), P(None, "rep"), P("blk", None)),
        check_vma=False,
    )
```
